256 devices in a mesh: grp: 8 (over z_lo, y), seq: 32 (over x, z_hi, core).
Axes of the slice: x: 4, y: 4, z: 8 (z_hi: 4, z_lo: 2; z = z_hi * 2 + z_lo), core: 2. Of those that a mesh axis runs over, the one named last changes fastest.
Arguments:
- queries: bfloat16 [32768, 1024], P(('grp', 'seq'))
- keys: bfloat16 [32768, 1024], P(('grp', 'seq'))
- values: bfloat16 [32768, 1024], P(('grp', 'seq')), may hold values from -6 to 6
- cotangent: bfloat16 [32768, 1024], P(('grp', 'seq')), may hold values from -6 to 6
- head_offsets: int32 [4, 8], replicated, may hold values from 0 to 7, as said below
- level_bias: float32 [4, 8], replicated, may hold values from -1.5 to 1.5
Outputs:
- attended: bfloat16 [32768, 1024], P(('grp', 'seq'))
- query_grad: bfloat16 [32768, 1024], P(('grp', 'seq'))
- key_grad: bfloat16 [32768, 1024], P(('grp', 'seq'))
- value_grad: bfloat16 [32768, 1024], P(('grp', 'seq'))
- bias_grad: float32 [4, 8], replicated
The draws below stay inside these ranges and needn't reach their ends.
Inputs may be any that keep to these rules, and one draw needn't show every extreme that they name: head_offsets[l, h] lies in 0 to 2**l - 1.
All inputs are finite; a program needn't handle non-finite values.
Results may differ from the reference program's by a relative error of at most 0.025.
Values may be sent and summed in bfloat16 or wider, within the bound.
No kernel may reach another device: no remote copies, remote signals or barrier semaphores. Data moves between devices by JAX's collectives and lax.ppermute only.
A program may use at most 128 MiB of HBM per device.

```python
import jax
import jax.numpy as jnp
from jax import lax

H = 8
HD = 128
KEEP = 256
LEVELS = 4
D = 1024
SEQLEN = 4096
TOKENS = 32768


def key_field(key):
    field = jax.random.normal(jax.random.fold_in(key, 11), (TOKENS, D), jnp.float32)
    return jnp.clip(field, -5.0, 5.0)


def draw_keys(key, part):
    field = key_field(key)
    return field.astype(jnp.bfloat16)


def draw_queries(key, part):
    key = jax.random.fold_in(key, 5)
    drawn = jnp.clip(jax.random.normal(key, (TOKENS, D), jnp.float32), -5.0, 5.0)
    return drawn.astype(jnp.bfloat16)


def draw_head_offsets(key, part):
    key = jax.random.fold_in(key, 9)
    start = jax.random.randint(key, (LEVELS, 1), 0, 2 ** LEVELS)
    heads = jnp.arange(H, dtype=jnp.int32)[None, :]
    span = (2 ** jnp.arange(LEVELS, dtype=jnp.int32))[:, None]
    return ((start + heads) % span).astype(jnp.int32)


def block_scale(own_key, shape, cuts, low, high):
    loudness, own = 1.0, jax.random.fold_in(own_key, 6)
    for position, parts in cuts:
        steps = jnp.exp(jax.random.uniform(jax.random.fold_in(own, position), (parts,), jnp.float32, low / len(cuts), high / len(cuts)))
        loudness = loudness * jnp.repeat(steps, shape[position] // parts).reshape([-1 if axis == position else 1 for axis in range(len(shape))])
    return loudness


def scatter_about(own_key, dims, deviation, limit, shards=(), kind=jnp.bfloat16):
    array = jax.random.normal(own_key, dims, jnp.float32) * deviation
    if len(shards) > 0:
        array = block_scale(own_key, dims, shards, -0.22, 0.18) * array
    return jnp.clip(array, min=-limit, max=limit).astype(kind)


def setup_inputs(seed: int = 0) -> dict:
    seeds = jax.random.split(jax.random.key(seed), 7)
    queries = draw_queries(jax.random.fold_in(seeds[6], 71), 0)
    keys = draw_keys(jax.random.fold_in(seeds[6], 71), 0)
    values = scatter_about(seeds[2], (TOKENS, D), 1.0, 6.0, ((0, 256),))
    cotangent = scatter_about(seeds[3], (TOKENS, D), 1.0, 6.0, ((0, 256),))
    head_offsets = draw_head_offsets(jax.random.fold_in(seeds[6], 71), 0)
    level_bias = jnp.clip(jax.random.uniform(seeds[5], (LEVELS, H), jnp.float32, -1.5, 1.5), -1.5, 1.5)
    return {"queries": queries, "keys": keys, "values": values, "cotangent": cotangent, "head_offsets": head_offsets, "level_bias": level_bias}


def pick(x, r, offsets):
    onehot = (jnp.arange(r)[:, None] == offsets[None, :]).astype(x.dtype)
    shaped = x.reshape((x.shape[0] // r, r) + x.shape[1:])
    weight = onehot.reshape((1, r, onehot.shape[1]) + (1,) * (x.ndim - 2))
    return jnp.sum(shaped * weight, axis=1).astype(x.dtype)


def spread(x, r, offsets):
    onehot = (jnp.arange(r)[:, None] == offsets[None, :]).astype(x.dtype)
    weight = onehot.reshape((1, r, onehot.shape[1]) + (1,) * (x.ndim - 2))
    placed = x[:, None] * weight
    return placed.reshape((x.shape[0] * r,) + x.shape[1:])


def group_pass(args):
    queries, keys, values, cotangent, head_offsets, level_bias = args
    scale = HD ** -0.5
    q3 = queries.reshape(-1, H, HD)
    k3 = keys.reshape(-1, H, HD)
    v3 = values.reshape(-1, H, HD)
    d3 = cotangent.reshape(-1, H, HD).astype(jnp.float32)
    rows_all = q3.shape[0]
    saved = []
    placed_out = []
    logits = []
    for level in range(LEVELS):
        r = 2 ** level
        offs = head_offsets[level]
        qs = pick(q3, r, offs).reshape(-1, KEEP, H, HD)
        ks = pick(k3, r, offs).reshape(-1, KEEP, H, HD)
        vs = pick(v3, r, offs).reshape(-1, KEEP, H, HD)
        s = jnp.einsum("nqhd,nkhd->nhqk", qs.astype(jnp.float32), ks.astype(jnp.float32)) * scale
        lse = jax.nn.logsumexp(s, axis=-1)
        p = jnp.exp(s - lse[..., None])
        pb = p.astype(jnp.bfloat16)
        o = jnp.einsum("nhqk,nkhd->nqhd", pb.astype(jnp.float32), vs.astype(jnp.float32))
        saved.append((qs, ks, vs, p, pb, o))
        placed_out.append(spread(o.reshape(-1, H, HD), r, offs))
        kept = spread(jnp.ones((rows_all // r, H), jnp.float32), r, offs)
        lse_rows = jnp.transpose(lse, (0, 2, 1)).reshape(-1, H)
        logits.append(jnp.where(kept > 0, spread(lse_rows, r, offs) + level_bias[level][None, :], -jnp.inf))
    z = jnp.stack(logits)
    mix = jax.nn.softmax(z, axis=0)
    out = jnp.zeros((rows_all, H, HD), jnp.float32)
    for level in range(LEVELS):
        out = out + mix[level][..., None] * placed_out[level]
    attended = out.astype(jnp.bfloat16)
    dq_sum = jnp.zeros((rows_all, H, HD), jnp.float32)
    dk_sum = jnp.zeros((rows_all, H, HD), jnp.float32)
    dv_sum = jnp.zeros((rows_all, H, HD), jnp.float32)
    bias_rows = []
    for level in range(LEVELS):
        r = 2 ** level
        offs = head_offsets[level]
        qs, ks, vs, p, pb, o = saved[level]
        g = mix[level] * jnp.sum(d3 * (placed_out[level] - out), axis=-1)
        bias_rows.append(jnp.sum(g, axis=0))
        dob = pick(mix[level][..., None] * d3, r, offs).astype(jnp.bfloat16).reshape(-1, KEEP, H, HD)
        gsel = pick(g, r, offs).reshape(-1, KEEP, H)
        c = jnp.sum(dob.astype(jnp.float32) * o, axis=-1) - gsel
        dp = jnp.einsum("nqhd,nkhd->nhqk", dob.astype(jnp.float32), vs.astype(jnp.float32))
        ds = (p * (dp - jnp.transpose(c, (0, 2, 1))[..., None])).astype(jnp.bfloat16).astype(jnp.float32)
        dq = jnp.einsum("nhqk,nkhd->nqhd", ds, ks.astype(jnp.float32)) * scale
        dk = jnp.einsum("nhqk,nqhd->nkhd", ds, qs.astype(jnp.float32)) * scale
        dv = jnp.einsum("nhqk,nqhd->nkhd", pb.astype(jnp.float32), dob.astype(jnp.float32))
        dq_sum = dq_sum + spread(dq.reshape(-1, H, HD), r, offs)
        dk_sum = dk_sum + spread(dk.reshape(-1, H, HD), r, offs)
        dv_sum = dv_sum + spread(dv.reshape(-1, H, HD), r, offs)
    shape2 = (rows_all, H * HD)
    return (attended.reshape(shape2), dq_sum.astype(jnp.bfloat16).reshape(shape2),
            dk_sum.astype(jnp.bfloat16).reshape(shape2), dv_sum.astype(jnp.bfloat16).reshape(shape2),
            jnp.stack(bias_rows))


def reference(queries, keys, values, cotangent, head_offsets, level_bias):
    groups = queries.shape[0] // SEQLEN
    def regroup(x):
        return x.reshape(groups, SEQLEN, x.shape[1])
    def one(items):
        return group_pass((items[0], items[1], items[2], items[3], head_offsets, level_bias))
    att, dq, dk, dv, bias_grad = lax.map(one, (regroup(queries), regroup(keys), regroup(values), regroup(cotangent)))
    width = queries.shape[1]
    return (att.reshape(-1, width), dq.reshape(-1, width), dk.reshape(-1, width), dv.reshape(-1, width),
            jnp.sum(bias_grad, axis=0))
```

```python
import jax
import jax.numpy as jnp
from jax import lax
from jax.experimental import pallas as pl
from jax.experimental.pallas import tpu as pltpu
from jax.sharding import PartitionSpec as P

H = 8
HD = 128
LEVELS = 4
ROWS = 128
TILE = 16
BIG = 60 * 1024 * 1024
RES = 8
SCALE = HD ** (-0.5)
F32 = jnp.float32
BF16 = jnp.bfloat16
I32 = jnp.int32
VM = pl.BlockSpec(memory_space=pltpu.VMEM)
SM = pl.BlockSpec(memory_space=pltpu.SMEM)
PARAMS = pltpu.CompilerParams(vmem_limit_bytes=16 * 1024 * 1024)

SLOTS = [(dz, dc) for dz in range(4) for dc in range(2)]
CORE, FAR, FAR2 = 1, 4, 5
NEAR = [2, 6, 3, 7]
SEND = [CORE] + NEAR + [FAR, FAR2]

PER = [8, 4, 2, 1]
BASE = [0, 1024, 1536, 1792]
COMPACT = 1920


def z_perm(dz, dc):
    pairs = []
    for i in range(32):
        x, z, c = i // 8, i % 8 // 2, i % 2
        pairs.append((i, x * 8 + (z + dz) % 4 * 2 + (c ^ dc)))
    return pairs


def xor_perm(bits):
    return [(i, i ^ bits) for i in range(32)]


def dest_head(e, dz, dc):
    z = e // 2
    c = e - 2 * z
    return lax.rem(z + dz, 4) * 2 + (c if dc == 0 else 1 - c)


def dot_nn(a, b):
    return jnp.dot(a, b, preferred_element_type=F32)


def dot_nt(a, b):
    return lax.dot_general(a, b, (((1,), (1,)), ((), ())), preferred_element_type=F32)


def dot_tn(a, b):
    return lax.dot_general(a, b, (((0,), (0,)), ((), ())), preferred_element_type=F32)


def row_order(transposed):
    shape = (ROWS, ROWS)
    packed = lax.broadcasted_iota(I32, shape, 1 if transposed else 0)
    plain = lax.broadcasted_iota(I32, shape, 0 if transposed else 1)
    return (plain == (packed % TILE) * RES + packed // TILE).astype(BF16)


def tile_at(row):
    return pl.ds(pl.multiple_of(row, TILE), TILE)


def head_at(h):
    return pl.ds(pl.multiple_of(h * HD, HD), HD)


def shape(dtype, *dims):
    return jax.ShapeDtypeStruct(dims, dtype)


def call(kernel, outs, ins, out_specs, scratch=(), cost=None):
    return pl.pallas_call(
        kernel,
        out_shape=outs,
        in_specs=ins,
        out_specs=out_specs,
        scratch_shapes=list(scratch),
        compiler_params=PARAMS,
        cost_estimate=cost,
    )


def pack_kernel(offs, k, v, q, d, *rest):
    outs, info, tmp = rest[:8], rest[8], rest[9]
    e = lax.rem(lax.axis_index("seq"), 8)
    order = row_order(False)
    for level in range(LEVELS):
        info[level] = offs[level, e]
    info[4] = e
    for a, ref in enumerate((k, v, q, d)):
        tmp[...] = dot_nn(order, ref[...]).astype(BF16)
        for slot, (dz, dc) in enumerate(SLOTS):
            outs[slot][a] = tmp[:, head_at(dest_head(e, dz, dc))]


def pack(offs, k, v, q, d):
    return pl.pallas_call(
        pack_kernel,
        out_shape=[shape(BF16, 4, ROWS, HD)] * 8 + [shape(I32, 8)],
        in_specs=[SM] + [VM] * 4,
        out_specs=[VM] * 8 + [SM],
        scratch_shapes=[pltpu.VMEM((ROWS, H * HD), BF16)],
        compiler_params=pltpu.CompilerParams(vmem_limit_bytes=BIG),
    )(offs, k, v, q, d)


def by_slot(refs):
    return [refs[([0] + SEND).index(slot)] for slot in range(8)]


def in_order(got):
    return [got[slot] for slot in [0] + SEND]


def pick_kernel(info, *refs):
    got, out = by_slot(refs[:8]), refs[8]
    rows = tile_at(info[3] * TILE)
    for s in range(8):
        out[:, s * TILE : (s + 1) * TILE] = got[s][0:2, rows]


def pick3(info, got):
    return call(pick_kernel, shape(BF16, 2, ROWS, HD), [SM] + [VM] * 8, VM)(
        info, *in_order(got)
    )


def join(pieces):
    return pieces[0] if len(pieces) == 1 else jnp.concatenate(pieces, axis=0)


def load(ref, parts):
    return join([ref[pl.ds(start, size)] for start, size in parts])


def store(ref, parts, value):
    row = 0
    for start, size in parts:
        ref[pl.ds(start, size)] = value[row : row + size]
        row += size


def segments(e):
    mate = jnp.where(lax.rem(e // 2, 2) == 0, 3, 1)
    near = pl.multiple_of(BASE[1] + mate * 128, 128)
    far = pl.multiple_of(BASE[1] + (4 - mate) * 128, 128)
    segs = [(0, [(m * 256, 256)]) for m in range(4)]
    segs.append((1, [(BASE[1], 128), (near, 128)]))
    segs.append((1, [(BASE[1] + 256, 128), (far, 128)]))
    segs.append((2, [(BASE[2], 256)]))
    return segs


def kept(level, off):
    r = 1 << level
    return [s * ROWS + (off + r * t) * TILE for s in range(8) for t in range(PER[level])]


def wide(column):
    return jnp.broadcast_to(column, (column.shape[0], HD))


def twice(x):
    return jnp.concatenate([x, x], axis=1)


def row_sum(x):
    return wide(jnp.sum(x, axis=-1, keepdims=True))


def softmax_rows(q, k, v):
    s = dot_nt(q, k) * SCALE
    m = jnp.max(s, axis=-1, keepdims=True)
    p = jnp.exp(s - m)
    l = jnp.sum(p, axis=-1, keepdims=True)
    p = p * (1.0 / l)
    return p, wide(m + jnp.log(l)), dot_nn(p.astype(BF16), v)


def fwd_kernel(info, *refs):
    got = by_slot(refs[:8])
    comp, p_s, o_s, z_s = refs[8:]
    for a in range(4):
        for s in range(8):
            comp[a, s * ROWS : (s + 1) * ROWS] = got[s][a]
            for level in range(1, LEVELS):
                for t in range(PER[level]):
                    at = tile_at((info[level] + (1 << level) * t) * TILE)
                    row = BASE[level] + (s * PER[level] + t) * TILE
                    comp[a, row : row + TILE] = got[s][a, at]
    for level, parts in segments(info[4]):
        q, k, v = (load(comp.at[a], parts) for a in (2, 0, 1))
        p, lse, o = softmax_rows(q, k, v)
        store(p_s, parts, p)
        store(z_s, parts, lse)
        store(o_s, parts, o)


def forward(info, got):
    return call(
        fwd_kernel,
        [
            shape(BF16, 4, COMPACT, HD),
            shape(F32, BASE[3], 256),
            shape(F32, BASE[3], HD),
            shape(F32, BASE[3], HD),
        ],
        [SM] + [VM] * 8,
        [VM] * 4,
        cost=pl.CostEstimate(flops=250000000, bytes_accessed=6000000, transcendentals=460000),
    )(info, *in_order(got))


def mix_kernel(info, bias, comp, o_s, z_s, xkv, *refs):
    att, do_s, c_s, acc3, xout, bias_out, z_t, lz_s, d_s = refs
    e = info[4]
    offs = [info[level] for level in range(LEVELS)]
    last = slice(BASE[3], COMPACT)
    q3 = comp[2, last]
    k3 = jnp.concatenate([comp[0, last], xkv[0]], axis=0)
    v3 = jnp.concatenate([comp[1, last], xkv[1]], axis=0)
    p3, lse3, o3 = softmax_rows(q3, k3, v3)
    for level in range(LEVELS - 1):
        at = slice(BASE[level], BASE[level + 1])
        z_t[at] = z_s[at] + bias[level, e]
    z_t[last] = lse3 + bias[3, e]

    ninf = jnp.float32(-jnp.inf)
    for s in range(8):
        rows = slice(s * ROWS, (s + 1) * ROWS)
        zs = [z_t[rows]]
        os = [o_s[rows]]
        for level in range(1, LEVELS):
            r = 1 << level
            zp, op = [], []
            for rho in range(RES):
                row = BASE[level] + (s * PER[level] + rho // r) * TILE
                zp.append(jnp.where(offs[level] == rho % r, z_t[row : row + TILE], ninf))
                if level == 3:
                    op.append(o3[s * TILE : (s + 1) * TILE])
                else:
                    op.append(o_s[row : row + TILE])
            zs.append(join(zp))
            os.append(join(op))
        top = jnp.maximum(jnp.maximum(zs[0], zs[1]), jnp.maximum(zs[2], zs[3]))
        es = [jnp.exp(x - top) for x in zs]
        den = es[0] + es[1] + es[2] + es[3]
        inv = 1.0 / den
        out = (es[0] * inv) * os[0]
        for level in range(1, LEVELS):
            out = out + (es[level] * inv) * os[level]
        att[s] = out.astype(BF16)
        lz_s[rows] = top + jnp.log(den)
        d_s[rows] = row_sum(comp[3, rows].astype(F32) * out)

    lane = lax.broadcasted_iota(I32, (1, 128), 1)
    biases = jnp.zeros((1, 128), F32)
    for level in (3, 0, 1, 2):
        end = COMPACT if level == 3 else BASE[level + 1]
        span = slice(BASE[level], end)
        if level == 0:
            lz, dd = lz_s[span], d_s[span]
        else:
            places = kept(level, offs[level])
            lz = join([lz_s[tile_at(x)] for x in places])
            dd = join([d_s[tile_at(x)] for x in places])
        cot = comp[3, span].astype(F32)
        o = o3 if level == 3 else o_s[span]
        a = jnp.exp(z_t[span] - lz)
        do = (a * cot).astype(BF16)
        g = a * (row_sum(cot * o) - dd)
        c = row_sum(do.astype(F32) * o) - g
        total = jnp.sum(g, axis=0, keepdims=True)
        biases = biases + jnp.where(lane == level * H + e, total, 0.0)
        if level < 3:
            do_s[span] = do
            c_s[span] = c
            continue
        dp = dot_nt(do, v3)
        ds = (p3 * (dp - twice(c))).astype(BF16)
        acc3[0] = dot_nn(ds, k3) * SCALE
        for n, value in ((1, dot_tn(ds, q3) * SCALE), (2, dot_tn(p3.astype(BF16), do))):
            acc3[n] = value[:ROWS]
            xout[n - 1] = value[ROWS:].astype(BF16)
    bias_out[...] = biases


def mixing(info, bias, comp, o, z, xkv):
    return call(
        mix_kernel,
        [
            shape(BF16, 8, ROWS, HD),
            shape(BF16, BASE[3], HD),
            shape(F32, BASE[3], HD),
            shape(F32, 3, ROWS, HD),
            shape(BF16, 2, ROWS, HD),
            shape(F32, 1, 128),
        ],
        [SM, SM] + [VM] * 4,
        [VM] * 6,
        [
            pltpu.VMEM((COMPACT, HD), F32),
            pltpu.VMEM((1024, HD), F32),
            pltpu.VMEM((1024, HD), F32),
        ],
        cost=pl.CostEstimate(flops=50000000, bytes_accessed=6000000, transcendentals=40000),
    )(info, bias, comp, o, z, xkv)


def bwd_kernel(info, comp, p_s, do_s, c_s, acc3, att, *refs):
    msgs, own3, acc = refs[:8], refs[8], refs[9]
    offs = [info[level] for level in range(LEVELS)]
    for level, parts in segments(info[4]):
        q, k, v = (load(comp.at[a], parts) for a in (2, 0, 1))
        p, do = load(p_s, parts), load(do_s, parts)
        ds = (p * (dot_nt(do, v) - twice(load(c_s, parts)))).astype(BF16)
        dq = dot_nn(ds, k) * SCALE
        dk = dot_tn(ds, q) * SCALE
        dv = dot_tn(p.astype(BF16), do)
        for which, value in enumerate((dq, dk, dv)):
            if level == 0:
                acc[which, pl.ds(parts[0][0], 256)] = value
                continue
            row = 0
            for start, size in parts:
                for i in range(size // TILE):
                    s = (start - BASE[level]) // (TILE * PER[level]) + i // PER[level]
                    rho = offs[level] + (1 << level) * (i % PER[level])
                    at = tile_at(s * ROWS + rho * TILE)
                    acc[which, at] = acc[which, at] + value[row : row + TILE]
                    row += TILE
    for s in range(8):
        at = tile_at(s * ROWS + offs[3] * TILE)
        part = slice(s * TILE, (s + 1) * TILE)
        for which in range(3):
            total = acc[which, at] + acc3[which, part]
            acc[which, at] = total
            if which > 0:
                own3[which - 1, part] = total
    for s in range(8):
        msgs[s][0] = att[s]
        for which in range(3):
            msgs[s][1 + which] = acc[which, s * ROWS : (s + 1) * ROWS].astype(BF16)


MSG = shape(BF16, 4, ROWS, HD)


def backward(info, comp, p, do, c, acc3, att):
    return call(
        bwd_kernel,
        [MSG] * 8 + [shape(F32, 2, ROWS, HD)],
        [SM] + [VM] * 6,
        [VM] * 9,
        [pltpu.VMEM((3, 1024, HD), F32)],
        cost=pl.CostEstimate(flops=600000000, bytes_accessed=6000000, transcendentals=0),
    )(info, comp, p, do, c, acc3, att)


def merge_kernel(info, *refs):
    own3, xin, bias = refs[8:11]
    outs, spread = refs[11:19], refs[19]
    for s in range(8):
        at = slice(s * TILE, (s + 1) * TILE)
        outs[s][...] = (own3[:, at] + xin[:, at].astype(F32)).astype(BF16)
    spread[...] = jnp.broadcast_to(bias[:, : LEVELS * H], spread.shape)


def merge(info, msgs, own3, xin, bias, devices):
    tile = pl.BlockSpec((2, TILE, HD), lambda i, info: (1, info[3], 0))

    def full(*dims):
        return pl.BlockSpec(dims, lambda i, info: (0,) * len(dims))

    rows = full(2, ROWS, HD)
    return pl.pallas_call(
        merge_kernel,
        out_shape=[MSG] * 8 + [shape(F32, devices, LEVELS * H)],
        grid_spec=pltpu.PrefetchScalarGridSpec(
            num_scalar_prefetch=1,
            grid=(1,),
            in_specs=[pl.BlockSpec(memory_space=pl.ANY)] * 8 + [rows, rows, full(1, 128)],
            out_specs=[tile] * 8 + [full(devices, LEVELS * H)],
        ),
        input_output_aliases={1 + n: n for n in range(8)},
        compiler_params=PARAMS,
    )(info, *msgs, own3, xin, bias)


def unpack_kernel(info, *refs):
    got, bias = by_slot(refs[:8]), refs[8]
    outs, bias_out = refs[9:13], refs[13]
    e = info[4]
    order = row_order(True)
    for a in range(4):
        for slot, (dz, dc) in enumerate(SLOTS):
            at = head_at(dest_head(e, dz, dc))
            outs[a][:, at] = dot_nn(order, got[slot][a]).astype(BF16)
    total = jnp.sum(bias[...], axis=0, keepdims=True)
    for level in range(LEVELS):
        bias_out[level : level + 1] = total[:, level * H : (level + 1) * H]


def unpack(info, got, bias):
    return call(
        unpack_kernel,
        [shape(BF16, ROWS, H * HD)] * 4 + [shape(F32, LEVELS, H)],
        [SM] + [VM] * 9,
        [VM] * 5,
    )(info, *in_order(got), bias)


def local(queries, keys, values, cotangent, head_offsets, level_bias):
    def move(x, pairs):
        return lax.ppermute(x, "seq", pairs)

    packed = pack(head_offsets, keys, values, queries, cotangent)
    sent, info = packed[:8], packed[8]
    got = [sent[0]] + [None] * 7
    for slot in SEND:
        got[slot] = move(sent[slot], z_perm(*SLOTS[slot]))
    xkv = move(pick3(info, got), xor_perm(8))
    comp, p, o, z = forward(info, got)
    att, do, c, acc3, xout, bias = mixing(info, level_bias, comp, o, z, xkv)
    xin = move(xout, xor_perm(8))
    *msgs, own3 = backward(info, comp, p, do, c, acc3, att)
    devices = lax.axis_size("grp") * lax.axis_size("seq")
    *msgs, spread = merge(info, msgs, own3, xin, bias, devices)
    back = [msgs[0]] + [None] * 7
    for slot in SEND:
        dz, dc = SLOTS[slot]
        back[slot] = move(msgs[slot], z_perm(-dz, dc))
    bias = lax.all_to_all(spread, ("grp", "seq"), 0, 0, tiled=True)
    return tuple(unpack(info, back, bias))


def solution(mesh):
    rows = P(("grp", "seq"), None)
    return jax.shard_map(
        local,
        mesh=mesh,
        in_specs=(rows, rows, rows, rows, P(), P()),
        out_specs=(rows, rows, rows, rows, P()),
        check_vma=False,
    )
```

```python
import jax
import jax.numpy as jnp
from jax import lax
from jax.experimental import pallas as pl
from jax.experimental.pallas import tpu as pltpu
from jax.sharding import PartitionSpec as P

H = 8
HD = 128
LEVELS = 4
ROWS = 128
TILE = 16
SHADOW = pl.CostEstimate(flops=0, bytes_accessed=200000000, transcendentals=0)
BIG = 53 * 1024 * 1024
RES = 8
SCALE = HD ** (-0.5)
F32 = jnp.float32
BF16 = jnp.bfloat16
I32 = jnp.int32
VM = pl.BlockSpec(memory_space=pltpu.VMEM)
SM = pl.BlockSpec(memory_space=pltpu.SMEM)
PARAMS = pltpu.CompilerParams(vmem_limit_bytes=16 * 1024 * 1024)

SLOTS = [(dz, dc) for dz in range(4) for dc in range(2)]
CORE, FAR, FAR2 = 1, 4, 5
NEAR = [2, 6, 3, 7]
SEND = [CORE] + NEAR + [FAR, FAR2]

PER = [8, 4, 2, 1]
BASE = [0, 1024, 1536, 1792]
COMPACT = 1920


GROUPS = [[g * 32 + i for g in range(8) for i in range(32) if i // 8 % 2 == n] for n in range(2)]


def z_perm(dz, dc):
    pairs = []
    for i in range(32):
        x, z, c = i // 8, i % 8 // 2, i % 2
        step = -dz if c ^ dc else dz
        pairs.append((i, x * 8 + (z + step) % 4 * 2 + (c ^ dc)))
    return pairs


def back_perm(dz, dc):
    return [(b, a) for a, b in z_perm(dz, dc)]


def xor_perm(bits):
    return [(i, i ^ bits) for i in range(32)]


def dest_head(e, dz, dc):
    z = e // 2
    c = e - 2 * z
    cd = c if dc == 0 else 1 - c
    return lax.rem(z + dz + cd * (4 - 2 * dz), 4) * 2 + cd


def dot_nn(a, b):
    return jnp.dot(a, b, preferred_element_type=F32)


def dot_nt(a, b):
    return lax.dot_general(a, b, (((1,), (1,)), ((), ())), preferred_element_type=F32)


def dot_tn(a, b):
    return lax.dot_general(a, b, (((0,), (0,)), ((), ())), preferred_element_type=F32)


def row_order(transposed):
    shape = (ROWS, ROWS)
    packed = lax.broadcasted_iota(I32, shape, 1 if transposed else 0)
    plain = lax.broadcasted_iota(I32, shape, 0 if transposed else 1)
    return (plain == (packed % TILE) * RES + packed // TILE).astype(BF16)


def tile_at(row):
    return pl.ds(pl.multiple_of(row, TILE), TILE)


def head_at(h):
    return pl.ds(pl.multiple_of(h * HD, HD), HD)


def shape(dtype, *dims):
    return jax.ShapeDtypeStruct(dims, dtype)


def call(kernel, outs, ins, out_specs, scratch=(), cost=None):
    return pl.pallas_call(
        kernel,
        out_shape=outs,
        in_specs=ins,
        out_specs=out_specs,
        scratch_shapes=list(scratch),
        compiler_params=PARAMS,
        cost_estimate=cost,
    )


def pack_kernel(k, v, q, d, *rest):
    outs, tmp = rest[:8], rest[8]
    e = lax.rem(lax.axis_index("seq"), 8)
    order = row_order(False)
    for a, ref in enumerate((k, v, q, d)):
        tmp[...] = dot_nn(order, ref[...]).astype(BF16)
        for slot, (dz, dc) in enumerate(SLOTS):
            outs[slot][a] = tmp[:, head_at(dest_head(e, dz, dc))]


def pack(k, v, q, d):
    return pl.pallas_call(
        pack_kernel,
        out_shape=[shape(BF16, 4, ROWS, HD)] * 8,
        in_specs=[VM] * 4,
        out_specs=[VM] * 8,
        scratch_shapes=[pltpu.VMEM((ROWS, H * HD), BF16)],
        compiler_params=pltpu.CompilerParams(vmem_limit_bytes=BIG),
    )(k, v, q, d)


def by_slot(refs):
    return [refs[([0] + SEND).index(slot)] for slot in range(8)]


def in_order(got):
    return [got[slot] for slot in [0] + SEND]


def pick_kernel(offs, *refs):
    got, out, info = by_slot(refs[:8]), refs[8], refs[9]
    e = lax.rem(lax.axis_index("seq"), 8)
    for level in range(LEVELS):
        info[level] = offs[level, e]
    info[4] = e
    rows = tile_at(offs[3, e] * TILE)
    for s in range(8):
        out[:, s * TILE : (s + 1) * TILE] = got[s][0:2, rows]


def pick3(offs, got):
    return call(
        pick_kernel,
        [shape(BF16, 2, ROWS, HD), shape(I32, 8)],
        [SM] + [VM] * 8,
        [VM, SM],
    )(offs, *in_order(got))


def join(pieces):
    return pieces[0] if len(pieces) == 1 else jnp.concatenate(pieces, axis=0)


def load(ref, parts):
    return join([ref[pl.ds(start, size)] for start, size in parts])


def store(ref, parts, value):
    row = 0
    for start, size in parts:
        ref[pl.ds(start, size)] = value[row : row + size]
        row += size


def segments(e):
    mate = jnp.where(lax.rem(e // 2 + e, 2) == 0, 3, 1)
    near = pl.multiple_of(BASE[1] + mate * 128, 128)
    far = pl.multiple_of(BASE[1] + (4 - mate) * 128, 128)
    segs = [(0, [(m * 256, 256)]) for m in range(4)]
    segs.append((1, [(BASE[1], 128), (near, 128)]))
    segs.append((1, [(BASE[1] + 256, 128), (far, 128)]))
    segs.append((2, [(BASE[2], 256)]))
    return segs


def kept(level, off):
    r = 1 << level
    return [s * ROWS + (off + r * t) * TILE for s in range(8) for t in range(PER[level])]


def wide(column):
    return jnp.broadcast_to(column, (column.shape[0], HD))


def twice(x):
    return jnp.concatenate([x, x], axis=1)


def row_sum(x):
    return wide(jnp.sum(x, axis=-1, keepdims=True))


def softmax_rows(q, k, v):
    s = dot_nt(q, k) * SCALE
    m = jnp.max(s, axis=-1, keepdims=True)
    p = jnp.exp(s - m)
    l = jnp.sum(p, axis=-1, keepdims=True)
    p = p * (1.0 / l)
    return p, wide(m + jnp.log(l)), dot_nn(p.astype(BF16), v)


def fwd_kernel(info, *refs):
    got = by_slot(refs[:8])
    comp, p_s, o_s, z_s = refs[8:]
    for a in range(4):
        for s in range(8):
            comp[a, s * ROWS : (s + 1) * ROWS] = got[s][a]
            for level in range(1, LEVELS):
                for t in range(PER[level]):
                    at = tile_at((info[level] + (1 << level) * t) * TILE)
                    row = BASE[level] + (s * PER[level] + t) * TILE
                    comp[a, row : row + TILE] = got[s][a, at]
    for level, parts in segments(info[4]):
        q, k, v = (load(comp.at[a], parts) for a in (2, 0, 1))
        p, lse, o = softmax_rows(q, k, v)
        store(p_s, parts, p)
        store(z_s, parts, lse)
        store(o_s, parts, o)


def forward(info, got):
    return call(
        fwd_kernel,
        [
            shape(BF16, 4, COMPACT, HD),
            shape(F32, BASE[3], 256),
            shape(F32, BASE[3], HD),
            shape(F32, BASE[3], HD),
        ],
        [SM] + [VM] * 8,
        [VM] * 4,
        cost=pl.CostEstimate(flops=250000000, bytes_accessed=6000000, transcendentals=460000),
    )(info, *in_order(got))


def mix_kernel(info, bias, comp, o_s, z_s, xkv, *refs):
    att, do_s, c_s, acc3, xout, bias_out, z_t, lz_s, d_s = refs
    e = info[4]
    offs = [info[level] for level in range(LEVELS)]
    last = slice(BASE[3], COMPACT)
    q3 = comp[2, last]
    k3 = jnp.concatenate([comp[0, last], xkv[0]], axis=0)
    v3 = jnp.concatenate([comp[1, last], xkv[1]], axis=0)
    p3, lse3, o3 = softmax_rows(q3, k3, v3)
    for level in range(LEVELS - 1):
        at = slice(BASE[level], BASE[level + 1])
        z_t[at] = z_s[at] + bias[level, e]
    z_t[last] = lse3 + bias[3, e]

    ninf = jnp.float32(-jnp.inf)
    for s in range(8):
        rows = slice(s * ROWS, (s + 1) * ROWS)
        zs = [z_t[rows]]
        os = [o_s[rows]]
        for level in range(1, LEVELS):
            r = 1 << level
            zp, op = [], []
            for rho in range(RES):
                row = BASE[level] + (s * PER[level] + rho // r) * TILE
                zp.append(jnp.where(offs[level] == rho % r, z_t[row : row + TILE], ninf))
                if level == 3:
                    op.append(o3[s * TILE : (s + 1) * TILE])
                else:
                    op.append(o_s[row : row + TILE])
            zs.append(join(zp))
            os.append(join(op))
        top = jnp.maximum(jnp.maximum(zs[0], zs[1]), jnp.maximum(zs[2], zs[3]))
        es = [jnp.exp(x - top) for x in zs]
        den = es[0] + es[1] + es[2] + es[3]
        inv = 1.0 / den
        out = (es[0] * inv) * os[0]
        for level in range(1, LEVELS):
            out = out + (es[level] * inv) * os[level]
        att[s] = out.astype(BF16)
        lz_s[rows] = top + jnp.log(den)
        d_s[rows] = row_sum(comp[3, rows].astype(F32) * out)

    lane = lax.broadcasted_iota(I32, (1, 128), 1)
    biases = jnp.zeros((1, 128), F32)
    for level in (3, 0, 1, 2):
        end = COMPACT if level == 3 else BASE[level + 1]
        span = slice(BASE[level], end)
        if level == 0:
            lz, dd = lz_s[span], d_s[span]
        else:
            places = kept(level, offs[level])
            lz = join([lz_s[tile_at(x)] for x in places])
            dd = join([d_s[tile_at(x)] for x in places])
        cot = comp[3, span].astype(F32)
        o = o3 if level == 3 else o_s[span]
        a = jnp.exp(z_t[span] - lz)
        do = (a * cot).astype(BF16)
        g = a * (row_sum(cot * o) - dd)
        c = row_sum(do.astype(F32) * o) - g
        total = jnp.sum(g, axis=0, keepdims=True)
        biases = biases + jnp.where(lane == level * H + e, total, 0.0)
        if level < 3:
            do_s[span] = do
            c_s[span] = c
            continue
        dp = dot_nt(do, v3)
        ds = (p3 * (dp - twice(c))).astype(BF16)
        acc3[0] = dot_nn(ds, k3) * SCALE
        for n, value in ((1, dot_tn(ds, q3) * SCALE), (2, dot_tn(p3.astype(BF16), do))):
            acc3[n] = value[:ROWS]
            xout[(n - 1) * ROWS : n * ROWS] = value[ROWS:].astype(BF16)
    bias_out[...] = biases
    high = biases.astype(BF16).astype(F32)
    middle = (biases - high).astype(BF16).astype(F32)
    row = lax.broadcasted_iota(I32, (TILE, 128), 0)
    terms = jnp.where(row == 0, high, jnp.where(row == 1, middle, biases - high - middle))
    xout[2 * ROWS :] = jnp.where(row < 3, terms, 0.0).astype(BF16)


def mixing(info, bias, comp, o, z, xkv):
    return call(
        mix_kernel,
        [
            shape(BF16, 8, ROWS, HD),
            shape(BF16, BASE[3], HD),
            shape(F32, BASE[3], HD),
            shape(F32, 3, ROWS, HD),
            shape(BF16, 2 * ROWS + TILE, HD),
            shape(F32, 1, 128),
        ],
        [SM, SM] + [VM] * 4,
        [VM] * 6,
        [
            pltpu.VMEM((COMPACT, HD), F32),
            pltpu.VMEM((1024, HD), F32),
            pltpu.VMEM((1024, HD), F32),
        ],
        cost=pl.CostEstimate(flops=50000000, bytes_accessed=6000000, transcendentals=40000),
    )(info, bias, comp, o, z, xkv)


def bwd_kernel(info, comp, p_s, do_s, c_s, acc3, att, *refs):
    own, zs, core, own3, acc = refs[0], refs[1:4], refs[4], refs[5], refs[6]
    offs = [info[level] for level in range(LEVELS)]
    for level, parts in segments(info[4]):
        q, k, v = (load(comp.at[a], parts) for a in (2, 0, 1))
        p, do = load(p_s, parts), load(do_s, parts)
        ds = (p * (dot_nt(do, v) - twice(load(c_s, parts)))).astype(BF16)
        dq = dot_nn(ds, k) * SCALE
        dk = dot_tn(ds, q) * SCALE
        dv = dot_tn(p.astype(BF16), do)
        for which, value in enumerate((dq, dk, dv)):
            if level == 0:
                acc[which, pl.ds(parts[0][0], 256)] = value
                continue
            row = 0
            for start, size in parts:
                for i in range(size // TILE):
                    s = (start - BASE[level]) // (TILE * PER[level]) + i // PER[level]
                    rho = offs[level] + (1 << level) * (i % PER[level])
                    at = tile_at(s * ROWS + rho * TILE)
                    acc[which, at] = acc[which, at] + value[row : row + TILE]
                    row += TILE
    for s in range(8):
        at = tile_at(s * ROWS + offs[3] * TILE)
        part = slice(s * TILE, (s + 1) * TILE)
        for which in range(3):
            total = acc[which, at] + acc3[which, part]
            acc[which, at] = total
            if which > 0:
                own3[which - 1, part] = total
    for s, (dz, dc) in enumerate(SLOTS):
        home = core.at[dz] if dc else (zs[dz - 1].at[0] if dz else own)
        home[0] = att[s]
        for which in range(3):
            home[1 + which] = acc[which, s * ROWS : (s + 1) * ROWS].astype(BF16)


MSGS = [shape(BF16, 4, ROWS, HD)] + [shape(BF16, 2, 4, ROWS, HD)] * 3
CORES = shape(BF16, 4, 4, ROWS, HD)


def backward(info, comp, p, do, c, acc3, att):
    return call(
        bwd_kernel,
        MSGS + [CORES, shape(F32, 2, ROWS, HD)],
        [SM] + [VM] * 6,
        [VM] * 6,
        [pltpu.VMEM((3, 1024, HD), F32)],
        cost=pl.CostEstimate(flops=600000000, bytes_accessed=6000000, transcendentals=0),
    )(info, comp, p, do, c, acc3, att)


def full(*dims):
    return pl.BlockSpec(dims, lambda i, info: (0,) * len(dims))


def patch(kernel, outs, blocks, ins, in_blocks, info):
    count = len(blocks)
    return pl.pallas_call(
        kernel,
        out_shape=outs,
        grid_spec=pltpu.PrefetchScalarGridSpec(
            num_scalar_prefetch=1,
            grid=(1,),
            in_specs=[pl.BlockSpec(memory_space=pl.ANY)] * count + in_blocks,
            out_specs=blocks + [full(*x.shape) for x in outs[count:]],
        ),
        input_output_aliases={1 + n: n for n in range(count)},
        compiler_params=PARAMS,
    )(info, *ins)


def merge_kernel(info, *refs):
    own3, xin, bias = refs[5:8]
    own, zs, core, bias_out = refs[8], refs[9:12], refs[12], refs[13]
    terms = jnp.sum(xin[2 * ROWS :].astype(F32), axis=0, keepdims=True)
    bias_out[...] = bias[...] + terms
    for s, (dz, dc) in enumerate(SLOTS):
        at = slice(s * TILE, (s + 1) * TILE)
        for a in range(2):
            theirs = xin[a * ROWS + s * TILE : a * ROWS + (s + 1) * TILE]
            total = (own3[a, at] + theirs.astype(F32)).astype(BF16)
            if dc:
                core[dz, a] = total
            elif dz:
                zs[dz - 1][0, a] = total
            else:
                own[a] = total


def merge(info, msgs, own3, xin, bias):
    one = pl.BlockSpec((2, TILE, HD), lambda i, info: (1, info[3], 0))
    two = pl.BlockSpec((1, 2, TILE, HD), lambda i, info: (0, 1, info[3], 0))
    four = pl.BlockSpec((4, 2, TILE, HD), lambda i, info: (0, 1, info[3], 0))
    return patch(
        merge_kernel,
        MSGS + [CORES, shape(F32, 1, 128)],
        [one, two, two, two, four],
        [*msgs, own3, xin, bias],
        [full(2, ROWS, HD), full(2 * ROWS + TILE, HD), full(1, 128)],
        info,
    )


def relay_kernel(info, *refs):
    core, bias = refs[3], refs[4]
    zs, spread = refs[5:8], refs[8]
    for dz in range(1, 4):
        zs[dz - 1][0] = core[4 - dz]
    spread[...] = jnp.broadcast_to(bias[:, : LEVELS * H], spread.shape)


def relay(info, msgs, core, bias, devices):
    half = pl.BlockSpec((1, 4, ROWS, HD), lambda i, info: (1, 0, 0, 0))
    return patch(
        relay_kernel,
        MSGS[1:] + [shape(F32, devices, LEVELS * H)],
        [half] * 3,
        [*msgs, core, bias],
        [full(*CORES.shape), full(1, 128)],
        info,
    )


def unpack_kernel(info, *refs):
    own, core = refs[0], refs[4]
    zs = [refs[1], refs[3], refs[2]]
    outs = refs[5:9]
    e = info[4]
    order = row_order(True)
    for a in range(4):
        for dz, dc in SLOTS:
            home = zs[3 - dz if dc else dz - 1].at[dc] if dz else (core.at[0] if dc else own)
            at = head_at(dest_head(e, dz, dc))
            outs[a][:, at] = dot_nn(order, home[a]).astype(BF16)


def total_kernel(bias, out):
    total = jnp.sum(bias[...], axis=0, keepdims=True)
    for level in range(LEVELS):
        out[level : level + 1] = total[:, level * H : (level + 1) * H]


def bias_total(bias):
    return call(total_kernel, shape(F32, LEVELS, H), [VM], VM)(bias)


def unpack(info, own, zs, core):
    return call(
        unpack_kernel,
        [shape(BF16, ROWS, H * HD)] * 4,
        [SM] + [VM] * 5,
        [VM] * 4,
        cost=SHADOW,
    )(info, own, zs[0], zs[2], zs[1], core)


def local(queries, keys, values, cotangent, head_offsets, level_bias):
    def move(x, pairs):
        return lax.ppermute(x, "seq", pairs)

    sent = pack(keys, values, queries, cotangent)
    got = [sent[0]] + [None] * 7
    for slot in SEND:
        got[slot] = move(sent[slot], z_perm(*SLOTS[slot]))
    picked, info = pick3(head_offsets, got)
    xkv = move(picked, xor_perm(8))
    comp, p, o, z = forward(info, got)
    att, do, c, acc3, xout, bias = mixing(info, level_bias, comp, o, z, xkv)
    xin = move(xout, xor_perm(8))
    *msgs, own3 = backward(info, comp, p, do, c, acc3, att)
    own, *zs, core, bias = merge(info, msgs, own3, xin, bias)
    core = move(core, xor_perm(1))
    *zs, spread = relay(info, zs, core, bias, 128)
    zs = [move(x, back_perm(dz, 0)) for dz, x in zip((1, 2, 3), zs)]
    bias = lax.all_to_all(
        spread, ("grp", "seq"), 0, 0, axis_index_groups=GROUPS, tiled=True
    )
    outs = unpack(info, own, zs, core)
    outs, bias = lax.optimization_barrier((outs, bias))
    return (*outs, bias_total(bias))


def solution(mesh):
    rows = P(("grp", "seq"), None)
    return jax.shard_map(
        local,
        mesh=mesh,
        in_specs=(rows, rows, rows, rows, P(), P()),
        out_specs=(rows, rows, rows, rows, P()),
        check_vma=False,
    )
```

```python
import jax
import jax.numpy as jnp
from jax import lax
from jax.experimental import pallas as pl
from jax.experimental.pallas import tpu as pltpu
from jax.sharding import PartitionSpec as P

H = 8
HD = 128
LEVELS = 4
ROWS = 128
TILE = 16
SHADOW = pl.CostEstimate(flops=0, bytes_accessed=200000000, transcendentals=0)
BIG = 53 * 1024 * 1024
RES = 8
SCALE = HD ** (-0.5)
F32 = jnp.float32
BF16 = jnp.bfloat16
I32 = jnp.int32
VM = pl.BlockSpec(memory_space=pltpu.VMEM)
SM = pl.BlockSpec(memory_space=pltpu.SMEM)
PARAMS = pltpu.CompilerParams(vmem_limit_bytes=16 * 1024 * 1024)

SLOTS = [(dz, dc) for dz in range(4) for dc in range(2)]
CORE, FAR, FAR2 = 1, 4, 5
NEAR = [2, 6, 3, 7]
SEND = [CORE] + NEAR + [FAR, FAR2]

PER = [8, 4, 2, 1]
BASE = [0, 1024, 1536, 1792]
COMPACT = 1920


GROUPS = [[g * 32 + i for g in range(8) for i in range(32) if i // 8 % 2 == n] for n in range(2)]


def z_perm(dz, dc):
    pairs = []
    for i in range(32):
        x, z, c = i // 8, i % 8 // 2, i % 2
        step = -dz if c ^ dc else dz
        pairs.append((i, x * 8 + (z + step) % 4 * 2 + (c ^ dc)))
    return pairs


def back_perm(dz, dc):
    return [(b, a) for a, b in z_perm(dz, dc)]


def xor_perm(bits):
    return [(i, i ^ bits) for i in range(32)]


def dest_head(e, dz, dc):
    z = e // 2
    c = e - 2 * z
    cd = c if dc == 0 else 1 - c
    return lax.rem(z + dz + cd * (4 - 2 * dz), 4) * 2 + cd


def dot_nn(a, b):
    return jnp.dot(a, b, preferred_element_type=F32)


def dot_nt(a, b):
    return lax.dot_general(a, b, (((1,), (1,)), ((), ())), preferred_element_type=F32)


def dot_tn(a, b):
    return lax.dot_general(a, b, (((0,), (0,)), ((), ())), preferred_element_type=F32)


def row_order(transposed):
    shape = (ROWS, ROWS)
    packed = lax.broadcasted_iota(I32, shape, 1 if transposed else 0)
    plain = lax.broadcasted_iota(I32, shape, 0 if transposed else 1)
    return (plain == (packed % TILE) * RES + packed // TILE).astype(BF16)


def tile_at(row):
    return pl.ds(pl.multiple_of(row, TILE), TILE)


def head_at(h):
    return pl.ds(pl.multiple_of(h * HD, HD), HD)


def shape(dtype, *dims):
    return jax.ShapeDtypeStruct(dims, dtype)


def call(kernel, outs, ins, out_specs, scratch=(), cost=None):
    return pl.pallas_call(
        kernel,
        out_shape=outs,
        in_specs=ins,
        out_specs=out_specs,
        scratch_shapes=list(scratch),
        compiler_params=PARAMS,
        cost_estimate=cost,
    )


def pack_kernel(offs, k, v, q, d, *rest):
    outs, info, tmp = rest[:8], rest[8], rest[9]
    e = lax.rem(lax.axis_index("seq"), 8)
    order = row_order(False)
    for level in range(LEVELS):
        info[level] = offs[level, e]
    info[4] = e
    info[5] = dest_head(e, 2, 0) // 2
    for a, ref in enumerate((k, v, q, d)):
        tmp[...] = dot_nn(order, ref[...]).astype(BF16)
        for slot, (dz, dc) in enumerate(SLOTS):
            outs[slot][a] = tmp[:, head_at(dest_head(e, dz, dc))]


def pack(offs, k, v, q, d):
    return pl.pallas_call(
        pack_kernel,
        out_shape=[shape(BF16, 4, ROWS, HD)] * 8 + [shape(I32, 8)],
        in_specs=[SM] + [VM] * 4,
        out_specs=[VM] * 8 + [SM],
        scratch_shapes=[pltpu.VMEM((ROWS, H * HD), BF16)],
        compiler_params=pltpu.CompilerParams(vmem_limit_bytes=BIG),
    )(offs, k, v, q, d)


def by_slot(refs):
    return [refs[([0] + SEND).index(slot)] for slot in range(8)]


def in_order(got):
    return [got[slot] for slot in [0] + SEND]


def pick_kernel(info, *refs):
    got, out = by_slot(refs[:8]), refs[8]
    rows = tile_at(info[3] * TILE)
    for s in range(8):
        out[:, s * TILE : (s + 1) * TILE] = got[s][0:2, rows]


def pick3(info, got):
    return call(pick_kernel, shape(BF16, 2, ROWS, HD), [SM] + [VM] * 8, VM)(
        info, *in_order(got)
    )


def join(pieces):
    return pieces[0] if len(pieces) == 1 else jnp.concatenate(pieces, axis=0)


def load(ref, parts):
    return join([ref[pl.ds(start, size)] for start, size in parts])


def store(ref, parts, value):
    row = 0
    for start, size in parts:
        ref[pl.ds(start, size)] = value[row : row + size]
        row += size


def segments(e):
    mate = jnp.where(lax.rem(e // 2 + e, 2) == 0, 3, 1)
    near = pl.multiple_of(BASE[1] + mate * 128, 128)
    far = pl.multiple_of(BASE[1] + (4 - mate) * 128, 128)
    segs = [(0, [(m * 256, 256)]) for m in range(4)]
    segs.append((1, [(BASE[1], 128), (near, 128)]))
    segs.append((1, [(BASE[1] + 256, 128), (far, 128)]))
    segs.append((2, [(BASE[2], 256)]))
    return segs


def kept(level, off):
    r = 1 << level
    return [s * ROWS + (off + r * t) * TILE for s in range(8) for t in range(PER[level])]


def wide(column):
    return jnp.broadcast_to(column, (column.shape[0], HD))


def twice(x):
    return jnp.concatenate([x, x], axis=1)


def row_sum(x):
    return wide(jnp.sum(x, axis=-1, keepdims=True))


def softmax_rows(q, k, v):
    s = dot_nt(q, k) * SCALE
    m = jnp.max(s, axis=-1, keepdims=True)
    p = jnp.exp(s - m)
    l = jnp.sum(p, axis=-1, keepdims=True)
    p = p * (1.0 / l)
    return p, wide(m + jnp.log(l)), dot_nn(p.astype(BF16), v)


def fwd_kernel(info, *refs):
    got = by_slot(refs[:8])
    comp, p_s, o_s, z_s = refs[8:]
    for a in range(4):
        for s in range(8):
            comp[a, s * ROWS : (s + 1) * ROWS] = got[s][a]
            for level in range(1, LEVELS):
                for t in range(PER[level]):
                    at = tile_at((info[level] + (1 << level) * t) * TILE)
                    row = BASE[level] + (s * PER[level] + t) * TILE
                    comp[a, row : row + TILE] = got[s][a, at]
    for level, parts in segments(info[4]):
        q, k, v = (load(comp.at[a], parts) for a in (2, 0, 1))
        p, lse, o = softmax_rows(q, k, v)
        store(p_s, parts, p)
        store(z_s, parts, lse)
        store(o_s, parts, o)


def forward(info, got):
    return call(
        fwd_kernel,
        [
            shape(BF16, 4, COMPACT, HD),
            shape(F32, BASE[3], 256),
            shape(F32, BASE[3], HD),
            shape(F32, BASE[3], HD),
        ],
        [SM] + [VM] * 8,
        [VM] * 4,
        cost=pl.CostEstimate(flops=250000000, bytes_accessed=6000000, transcendentals=460000),
    )(info, *in_order(got))


def mix_kernel(info, bias, comp, o_s, z_s, xkv, *refs):
    att, do_s, c_s, acc3, xout, bias_out, z_t, lz_s, d_s = refs
    e = info[4]
    offs = [info[level] for level in range(LEVELS)]
    last = slice(BASE[3], COMPACT)
    q3 = comp[2, last]
    k3 = jnp.concatenate([comp[0, last], xkv[0]], axis=0)
    v3 = jnp.concatenate([comp[1, last], xkv[1]], axis=0)
    p3, lse3, o3 = softmax_rows(q3, k3, v3)
    for level in range(LEVELS - 1):
        at = slice(BASE[level], BASE[level + 1])
        z_t[at] = z_s[at] + bias[level, e]
    z_t[last] = lse3 + bias[3, e]

    ninf = jnp.float32(-jnp.inf)
    for s in range(8):
        rows = slice(s * ROWS, (s + 1) * ROWS)
        zs = [z_t[rows]]
        os = [o_s[rows]]
        for level in range(1, LEVELS):
            r = 1 << level
            zp, op = [], []
            for rho in range(RES):
                row = BASE[level] + (s * PER[level] + rho // r) * TILE
                zp.append(jnp.where(offs[level] == rho % r, z_t[row : row + TILE], ninf))
                if level == 3:
                    op.append(o3[s * TILE : (s + 1) * TILE])
                else:
                    op.append(o_s[row : row + TILE])
            zs.append(join(zp))
            os.append(join(op))
        top = jnp.maximum(jnp.maximum(zs[0], zs[1]), jnp.maximum(zs[2], zs[3]))
        es = [jnp.exp(x - top) for x in zs]
        den = es[0] + es[1] + es[2] + es[3]
        inv = 1.0 / den
        out = (es[0] * inv) * os[0]
        for level in range(1, LEVELS):
            out = out + (es[level] * inv) * os[level]
        att[s] = out.astype(BF16)
        lz_s[rows] = top + jnp.log(den)
        d_s[rows] = row_sum(comp[3, rows].astype(F32) * out)

    lane = lax.broadcasted_iota(I32, (1, 128), 1)
    biases = jnp.zeros((1, 128), F32)
    for level in (3, 0, 1, 2):
        end = COMPACT if level == 3 else BASE[level + 1]
        span = slice(BASE[level], end)
        if level == 0:
            lz, dd = lz_s[span], d_s[span]
        else:
            places = kept(level, offs[level])
            lz = join([lz_s[tile_at(x)] for x in places])
            dd = join([d_s[tile_at(x)] for x in places])
        cot = comp[3, span].astype(F32)
        o = o3 if level == 3 else o_s[span]
        a = jnp.exp(z_t[span] - lz)
        do = (a * cot).astype(BF16)
        g = a * (row_sum(cot * o) - dd)
        c = row_sum(do.astype(F32) * o) - g
        total = jnp.sum(g, axis=0, keepdims=True)
        biases = biases + jnp.where(lane == level * H + e, total, 0.0)
        if level < 3:
            do_s[span] = do
            c_s[span] = c
            continue
        dp = dot_nt(do, v3)
        ds = (p3 * (dp - twice(c))).astype(BF16)
        acc3[0] = dot_nn(ds, k3) * SCALE
        for n, value in ((1, dot_tn(ds, q3) * SCALE), (2, dot_tn(p3.astype(BF16), do))):
            acc3[n] = value[:ROWS]
            xout[(n - 1) * ROWS : n * ROWS] = value[ROWS:].astype(BF16)
    bias_out[...] = biases
    high = biases.astype(BF16).astype(F32)
    middle = (biases - high).astype(BF16).astype(F32)
    row = lax.broadcasted_iota(I32, (TILE, 128), 0)
    terms = jnp.where(row == 0, high, jnp.where(row == 1, middle, biases - high - middle))
    xout[2 * ROWS :] = jnp.where(row < 3, terms, 0.0).astype(BF16)


def mixing(info, bias, comp, o, z, xkv):
    return call(
        mix_kernel,
        [
            shape(BF16, 8, ROWS, HD),
            shape(BF16, BASE[3], HD),
            shape(F32, BASE[3], HD),
            shape(F32, 3, ROWS, HD),
            shape(BF16, 2 * ROWS + TILE, HD),
            shape(F32, 1, 128),
        ],
        [SM, SM] + [VM] * 4,
        [VM] * 6,
        [
            pltpu.VMEM((COMPACT, HD), F32),
            pltpu.VMEM((1024, HD), F32),
            pltpu.VMEM((1024, HD), F32),
        ],
        cost=pl.CostEstimate(flops=50000000, bytes_accessed=6000000, transcendentals=40000),
    )(info, bias, comp, o, z, xkv)


def bwd_kernel(info, comp, p_s, do_s, c_s, acc3, att, *refs):
    own, zs, core, own3, acc = refs[0], refs[1:4], refs[4], refs[5], refs[6]
    offs = [info[level] for level in range(LEVELS)]
    for level, parts in segments(info[4]):
        q, k, v = (load(comp.at[a], parts) for a in (2, 0, 1))
        p, do = load(p_s, parts), load(do_s, parts)
        ds = (p * (dot_nt(do, v) - twice(load(c_s, parts)))).astype(BF16)
        dq = dot_nn(ds, k) * SCALE
        dk = dot_tn(ds, q) * SCALE
        dv = dot_tn(p.astype(BF16), do)
        for which, value in enumerate((dq, dk, dv)):
            if level == 0:
                acc[which, pl.ds(parts[0][0], 256)] = value
                continue
            row = 0
            for start, size in parts:
                for i in range(size // TILE):
                    s = (start - BASE[level]) // (TILE * PER[level]) + i // PER[level]
                    rho = offs[level] + (1 << level) * (i % PER[level])
                    at = tile_at(s * ROWS + rho * TILE)
                    acc[which, at] = acc[which, at] + value[row : row + TILE]
                    row += TILE
    for s in range(8):
        at = tile_at(s * ROWS + offs[3] * TILE)
        part = slice(s * TILE, (s + 1) * TILE)
        for which in range(3):
            total = acc[which, at] + acc3[which, part]
            acc[which, at] = total
            if which > 0:
                own3[which - 1, part] = total
    for s, (dz, dc) in enumerate(SLOTS):
        home = core.at[dz] if dc else (zs[dz - 1].at[0] if dz else own)
        home[0] = att[s]
        for which in range(3):
            home[1 + which] = acc[which, s * ROWS : (s + 1) * ROWS].astype(BF16)


MSGS = [shape(BF16, 4, ROWS, HD)] + [shape(BF16, 2, 4, ROWS, HD)] * 3
CORES = shape(BF16, 4, 4, ROWS, HD)


def backward(info, comp, p, do, c, acc3, att):
    return call(
        bwd_kernel,
        MSGS + [CORES, shape(F32, 2, ROWS, HD)],
        [SM] + [VM] * 6,
        [VM] * 6,
        [pltpu.VMEM((3, 1024, HD), F32)],
        cost=pl.CostEstimate(flops=600000000, bytes_accessed=6000000, transcendentals=0),
    )(info, comp, p, do, c, acc3, att)


def full(*dims):
    return pl.BlockSpec(dims, lambda i, info: (0,) * len(dims))


def patch(kernel, outs, blocks, ins, in_blocks, info):
    count = len(blocks)
    return pl.pallas_call(
        kernel,
        out_shape=outs,
        grid_spec=pltpu.PrefetchScalarGridSpec(
            num_scalar_prefetch=1,
            grid=(1,),
            in_specs=[pl.BlockSpec(memory_space=pl.ANY)] * count + in_blocks,
            out_specs=blocks + [full(*x.shape) for x in outs[count:]],
        ),
        input_output_aliases={1 + n: n for n in range(count)},
        compiler_params=PARAMS,
    )(info, *ins)


def merge_kernel(info, *refs):
    own3, xin, bias = refs[5:8]
    own, zs, core, bias_out = refs[8], refs[9:12], refs[12], refs[13]
    terms = jnp.sum(xin[2 * ROWS :].astype(F32), axis=0, keepdims=True)
    bias_out[...] = bias[...] + terms
    for s, (dz, dc) in enumerate(SLOTS):
        at = slice(s * TILE, (s + 1) * TILE)
        for a in range(2):
            theirs = xin[a * ROWS + s * TILE : a * ROWS + (s + 1) * TILE]
            total = (own3[a, at] + theirs.astype(F32)).astype(BF16)
            if dc:
                core[dz, a] = total
            elif dz:
                zs[dz - 1][0, a] = total
            else:
                own[a] = total


def merge(info, msgs, own3, xin, bias):
    one = pl.BlockSpec((2, TILE, HD), lambda i, info: (1, info[3], 0))
    two = pl.BlockSpec((1, 2, TILE, HD), lambda i, info: (0, 1, info[3], 0))
    four = pl.BlockSpec((4, 2, TILE, HD), lambda i, info: (0, 1, info[3], 0))
    return patch(
        merge_kernel,
        MSGS + [CORES, shape(F32, 1, 128)],
        [one, two, two, two, four],
        [*msgs, own3, xin, bias],
        [full(2, ROWS, HD), full(2 * ROWS + TILE, HD), full(1, 128)],
        info,
    )


def relay_kernel(info, *refs):
    core, bias = refs[3], refs[4]
    zs, spread = refs[5:8], refs[8]
    for dz in range(1, 4):
        zs[dz - 1][0] = core[4 - dz]
    spread[...] = jnp.broadcast_to(bias[:, : LEVELS * H], spread.shape)


def relay(info, msgs, core, bias, devices):
    half = pl.BlockSpec((1, 4, ROWS, HD), lambda i, info: (1, 0, 0, 0))
    return patch(
        relay_kernel,
        MSGS[1:] + [shape(F32, devices, LEVELS * H)],
        [half] * 3,
        [*msgs, core, bias],
        [full(*CORES.shape), full(1, 128)],
        info,
    )


def unpack_kernel(info, *refs):
    own, core = refs[0], refs[4]
    zs = [refs[2], refs[1], refs[3]]
    outs = refs[5:9]
    e = info[4]
    order = row_order(True)
    for a in range(4):
        for dz, dc in SLOTS:
            home = zs[3 - dz if dc else dz - 1].at[dc] if dz else (core.at[0] if dc else own)
            at = head_at(dest_head(e, dz, dc))
            outs[a][:, at] = dot_nn(order, home[a]).astype(BF16)


def total_kernel(bias, out):
    total = jnp.sum(bias[...], axis=0, keepdims=True)
    for level in range(LEVELS):
        out[level : level + 1] = total[:, level * H : (level + 1) * H]


def bias_total(bias):
    return call(total_kernel, shape(F32, LEVELS, H), [VM], VM)(bias)


def unpack(info, own, zs, core):
    return call(
        unpack_kernel,
        [shape(BF16, ROWS, H * HD)] * 4,
        [SM] + [VM] * 5,
        [VM] * 4,
        cost=SHADOW,
    )(info, own, zs[1], zs[0], zs[2], core)


def local(queries, keys, values, cotangent, head_offsets, level_bias):
    def move(x, pairs):
        return lax.ppermute(x, "seq", pairs)

    packed = pack(head_offsets, keys, values, queries, cotangent)
    sent, info = packed[:8], packed[8]
    got = [sent[0]] + [None] * 7
    for slot in SEND:
        got[slot] = move(sent[slot], z_perm(*SLOTS[slot]))
    xkv = move(pick3(info, got), xor_perm(8))
    comp, p, o, z = forward(info, got)
    att, do, c, acc3, xout, bias = mixing(info, level_bias, comp, o, z, xkv)
    xin = move(xout, xor_perm(8))
    *msgs, own3 = backward(info, comp, p, do, c, acc3, att)
    own, *zs, core, bias = merge(info, msgs, own3, xin, bias)
    core = move(core, xor_perm(1))
    *zs, spread = relay(info, zs, core, bias, 128)
    zs = [move(x, back_perm(dz, 0)) for dz, x in zip((1, 2, 3), zs)]
    bias = lax.all_to_all(
        spread, ("grp", "seq"), 0, 0, axis_index_groups=GROUPS, tiled=True
    )
    outs = unpack(info, own, zs, core)
    outs, bias = lax.optimization_barrier((outs, bias))
    return (*outs, bias_total(bias))


def solution(mesh):
    rows = P(("grp", "seq"), None)
    return jax.shard_map(
        local,
        mesh=mesh,
        in_specs=(rows, rows, rows, rows, P(), P()),
        out_specs=(rows, rows, rows, rows, P()),
        check_vma=False,
    )
```

```python
import jax
import jax.numpy as jnp
from jax import lax
from jax.experimental import pallas as pl
from jax.experimental.pallas import tpu as pltpu
from jax.sharding import PartitionSpec as P

H = 8
HD = 128
LEVELS = 4
ROWS = 128
TILE = 16
SHADOW = pl.CostEstimate(flops=0, bytes_accessed=200000000, transcendentals=0)
BIG = 53 * 1024 * 1024
RES = 8
SCALE = HD ** (-0.5)
F32 = jnp.float32
BF16 = jnp.bfloat16
I32 = jnp.int32
VM = pl.BlockSpec(memory_space=pltpu.VMEM)
SM = pl.BlockSpec(memory_space=pltpu.SMEM)
PARAMS = pltpu.CompilerParams(vmem_limit_bytes=16 * 1024 * 1024)

SLOTS = [(dz, dc) for dz in range(4) for dc in range(2)]
CORE, FAR, FAR2 = 1, 4, 5
NEAR = [2, 6, 3, 7]
SEND = [CORE] + NEAR + [FAR, FAR2]

PER = [8, 4, 2, 1]
BASE = [0, 1024, 1536, 1792]
COMPACT = 1920


GROUPS = [
    [g * 32 + i for g in range(8) for i in range(32) if (i // 8 % 2, i % 2) == (n, core)]
    for n in range(2)
    for core in range(2)
]


def z_perm(dz, dc):
    pairs = []
    for i in range(32):
        x, z, c = i // 8, i % 8 // 2, i % 2
        step = -dz if c ^ dc else dz
        pairs.append((i, x * 8 + (z + step) % 4 * 2 + (c ^ dc)))
    return pairs


def back_perm(dz, dc):
    return [(b, a) for a, b in z_perm(dz, dc)]


def xor_perm(bits):
    return [(i, i ^ bits) for i in range(32)]


def dest_head(e, dz, dc):
    z = e // 2
    c = e - 2 * z
    cd = c if dc == 0 else 1 - c
    return lax.rem(z + dz + cd * (4 - 2 * dz), 4) * 2 + cd


def dot_nn(a, b):
    return jnp.dot(a, b, preferred_element_type=F32)


def dot_nt(a, b):
    return lax.dot_general(a, b, (((1,), (1,)), ((), ())), preferred_element_type=F32)


def dot_tn(a, b):
    return lax.dot_general(a, b, (((0,), (0,)), ((), ())), preferred_element_type=F32)


def row_order(transposed):
    shape = (ROWS, ROWS)
    packed = lax.broadcasted_iota(I32, shape, 1 if transposed else 0)
    plain = lax.broadcasted_iota(I32, shape, 0 if transposed else 1)
    return (plain == (packed % TILE) * RES + packed // TILE).astype(BF16)


def tile_at(row):
    return pl.ds(pl.multiple_of(row, TILE), TILE)


def head_at(h):
    return pl.ds(pl.multiple_of(h * HD, HD), HD)


def shape(dtype, *dims):
    return jax.ShapeDtypeStruct(dims, dtype)


def call(kernel, outs, ins, out_specs, scratch=(), cost=None):
    return pl.pallas_call(
        kernel,
        out_shape=outs,
        in_specs=ins,
        out_specs=out_specs,
        scratch_shapes=list(scratch),
        compiler_params=PARAMS,
        cost_estimate=cost,
    )


def pack_kernel(offs, k, v, q, d, *rest):
    outs, info, tmp = rest[:8], rest[8], rest[9]
    e = lax.rem(lax.axis_index("seq"), 8)
    order = row_order(False)
    for level in range(LEVELS):
        info[level] = offs[level, e]
    info[4] = e
    info[5] = dest_head(e, 2, 0) // 2
    for a, ref in enumerate((k, v, q, d)):
        tmp[...] = dot_nn(order, ref[...]).astype(BF16)
        for slot, (dz, dc) in enumerate(SLOTS):
            outs[slot][a] = tmp[:, head_at(dest_head(e, dz, dc))]


def pack(offs, k, v, q, d):
    return pl.pallas_call(
        pack_kernel,
        out_shape=[shape(BF16, 4, ROWS, HD)] * 8 + [shape(I32, 8)],
        in_specs=[SM] + [VM] * 4,
        out_specs=[VM] * 8 + [SM],
        scratch_shapes=[pltpu.VMEM((ROWS, H * HD), BF16)],
        compiler_params=pltpu.CompilerParams(vmem_limit_bytes=BIG),
    )(offs, k, v, q, d)


def by_slot(refs):
    return [refs[([0] + SEND).index(slot)] for slot in range(8)]


def in_order(got):
    return [got[slot] for slot in [0] + SEND]


def pick_kernel(info, *refs):
    got, out = by_slot(refs[:8]), refs[8]
    rows = tile_at(info[3] * TILE)
    for s in range(8):
        out[:, s * TILE : (s + 1) * TILE] = got[s][0:2, rows]


def pick3(info, got):
    return call(pick_kernel, shape(BF16, 2, ROWS, HD), [SM] + [VM] * 8, VM)(
        info, *in_order(got)
    )


def join(pieces):
    return pieces[0] if len(pieces) == 1 else jnp.concatenate(pieces, axis=0)


def load(ref, parts):
    return join([ref[pl.ds(start, size)] for start, size in parts])


def store(ref, parts, value):
    row = 0
    for start, size in parts:
        ref[pl.ds(start, size)] = value[row : row + size]
        row += size


def segments(e):
    mate = jnp.where(lax.rem(e // 2 + e, 2) == 0, 3, 1)
    near = pl.multiple_of(BASE[1] + mate * 128, 128)
    far = pl.multiple_of(BASE[1] + (4 - mate) * 128, 128)
    segs = [(0, [(m * 256, 256)]) for m in range(4)]
    segs.append((1, [(BASE[1], 128), (near, 128)]))
    segs.append((1, [(BASE[1] + 256, 128), (far, 128)]))
    segs.append((2, [(BASE[2], 256)]))
    return segs


def kept(level, off):
    r = 1 << level
    return [s * ROWS + (off + r * t) * TILE for s in range(8) for t in range(PER[level])]


def wide(column):
    return jnp.broadcast_to(column, (column.shape[0], HD))


def twice(x):
    return jnp.concatenate([x, x], axis=1)


def row_sum(x):
    return wide(jnp.sum(x, axis=-1, keepdims=True))


def softmax_rows(q, k, v):
    s = dot_nt(q, k) * SCALE
    m = jnp.max(s, axis=-1, keepdims=True)
    p = jnp.exp(s - m)
    l = jnp.sum(p, axis=-1, keepdims=True)
    p = p * (1.0 / l)
    return p, wide(m + jnp.log(l)), dot_nn(p.astype(BF16), v)


def fwd_kernel(info, *refs):
    got = by_slot(refs[:8])
    comp, p_s, o_s, z_s = refs[8:]
    for a in range(4):
        for s in range(8):
            comp[a, s * ROWS : (s + 1) * ROWS] = got[s][a]
            for level in range(1, LEVELS):
                for t in range(PER[level]):
                    at = tile_at((info[level] + (1 << level) * t) * TILE)
                    row = BASE[level] + (s * PER[level] + t) * TILE
                    comp[a, row : row + TILE] = got[s][a, at]
    for level, parts in segments(info[4]):
        q, k, v = (load(comp.at[a], parts) for a in (2, 0, 1))
        p, lse, o = softmax_rows(q, k, v)
        store(p_s, parts, p)
        store(z_s, parts, lse)
        store(o_s, parts, o)


def forward(info, got):
    return call(
        fwd_kernel,
        [
            shape(BF16, 4, COMPACT, HD),
            shape(F32, BASE[3], 256),
            shape(F32, BASE[3], HD),
            shape(F32, BASE[3], HD),
        ],
        [SM] + [VM] * 8,
        [VM] * 4,
        cost=pl.CostEstimate(flops=250000000, bytes_accessed=6000000, transcendentals=460000),
    )(info, *in_order(got))


def mix_kernel(info, bias, comp, o_s, z_s, xkv, *refs):
    att, do_s, c_s, acc3, xout, bias_out, z_t, lz_s, d_s = refs
    e = info[4]
    offs = [info[level] for level in range(LEVELS)]
    last = slice(BASE[3], COMPACT)
    q3 = comp[2, last]
    k3 = jnp.concatenate([comp[0, last], xkv[0]], axis=0)
    v3 = jnp.concatenate([comp[1, last], xkv[1]], axis=0)
    p3, lse3, o3 = softmax_rows(q3, k3, v3)
    for level in range(LEVELS - 1):
        at = slice(BASE[level], BASE[level + 1])
        z_t[at] = z_s[at] + bias[level, e]
    z_t[last] = lse3 + bias[3, e]

    ninf = jnp.float32(-jnp.inf)
    for s in range(8):
        rows = slice(s * ROWS, (s + 1) * ROWS)
        zs = [z_t[rows]]
        os = [o_s[rows]]
        for level in range(1, LEVELS):
            r = 1 << level
            zp, op = [], []
            for rho in range(RES):
                row = BASE[level] + (s * PER[level] + rho // r) * TILE
                zp.append(jnp.where(offs[level] == rho % r, z_t[row : row + TILE], ninf))
                if level == 3:
                    op.append(o3[s * TILE : (s + 1) * TILE])
                else:
                    op.append(o_s[row : row + TILE])
            zs.append(join(zp))
            os.append(join(op))
        top = jnp.maximum(jnp.maximum(zs[0], zs[1]), jnp.maximum(zs[2], zs[3]))
        es = [jnp.exp(x - top) for x in zs]
        den = es[0] + es[1] + es[2] + es[3]
        inv = 1.0 / den
        out = (es[0] * inv) * os[0]
        for level in range(1, LEVELS):
            out = out + (es[level] * inv) * os[level]
        att[s] = out.astype(BF16)
        lz_s[rows] = top + jnp.log(den)
        d_s[rows] = row_sum(comp[3, rows].astype(F32) * out)

    lane = lax.broadcasted_iota(I32, (1, 128), 1)
    biases = jnp.zeros((1, 128), F32)
    for level in (3, 0, 1, 2):
        end = COMPACT if level == 3 else BASE[level + 1]
        span = slice(BASE[level], end)
        if level == 0:
            lz, dd = lz_s[span], d_s[span]
        else:
            places = kept(level, offs[level])
            lz = join([lz_s[tile_at(x)] for x in places])
            dd = join([d_s[tile_at(x)] for x in places])
        cot = comp[3, span].astype(F32)
        o = o3 if level == 3 else o_s[span]
        a = jnp.exp(z_t[span] - lz)
        do = (a * cot).astype(BF16)
        g = a * (row_sum(cot * o) - dd)
        c = row_sum(do.astype(F32) * o) - g
        total = jnp.sum(g, axis=0, keepdims=True)
        biases = biases + jnp.where(lane == level * H + e, total, 0.0)
        if level < 3:
            do_s[span] = do
            c_s[span] = c
            continue
        dp = dot_nt(do, v3)
        ds = (p3 * (dp - twice(c))).astype(BF16)
        acc3[0] = dot_nn(ds, k3) * SCALE
        both = dot_tn(
            jnp.concatenate([ds, p3.astype(BF16)], axis=1),
            jnp.concatenate([q3, do], axis=1),
        )
        for n, value in ((1, both[:256, :HD] * SCALE), (2, both[256:, HD:])):
            acc3[n] = value[:ROWS]
            xout[(n - 1) * ROWS : n * ROWS] = value[ROWS:].astype(BF16)
    bias_out[...] = biases
    high = biases.astype(BF16).astype(F32)
    middle = (biases - high).astype(BF16).astype(F32)
    row = lax.broadcasted_iota(I32, (TILE, 128), 0)
    terms = jnp.where(row == 0, high, jnp.where(row == 1, middle, biases - high - middle))
    xout[2 * ROWS :] = jnp.where(row < 3, terms, 0.0).astype(BF16)


def mixing(info, bias, comp, o, z, xkv):
    return call(
        mix_kernel,
        [
            shape(BF16, 8, ROWS, HD),
            shape(BF16, BASE[3], HD),
            shape(F32, BASE[3], HD),
            shape(F32, 3, ROWS, HD),
            shape(BF16, 2 * ROWS + TILE, HD),
            shape(F32, 1, 128),
        ],
        [SM, SM] + [VM] * 4,
        [VM] * 6,
        [
            pltpu.VMEM((COMPACT, HD), F32),
            pltpu.VMEM((1024, HD), F32),
            pltpu.VMEM((1024, HD), F32),
        ],
        cost=pl.CostEstimate(flops=50000000, bytes_accessed=6000000, transcendentals=40000),
    )(info, bias, comp, o, z, xkv)


def bwd_kernel(info, comp, p_s, do_s, c_s, acc3, att, *refs):
    own, zs, core, own3, acc = refs[0], refs[1:4], refs[4], refs[5], refs[6]
    offs = [info[level] for level in range(LEVELS)]
    for level, parts in segments(info[4]):
        q, k, v = (load(comp.at[a], parts) for a in (2, 0, 1))
        p, do = load(p_s, parts), load(do_s, parts)
        ds = (p * (dot_nt(do, v) - twice(load(c_s, parts)))).astype(BF16)
        dq = dot_nn(ds, k) * SCALE
        both = dot_tn(
            jnp.concatenate([ds, p.astype(BF16)], axis=1),
            jnp.concatenate([q, do], axis=1),
        )
        dk = both[:256, :HD] * SCALE
        dv = both[256:, HD:]
        for which, value in enumerate((dq, dk, dv)):
            if level == 0:
                acc[which, pl.ds(parts[0][0], 256)] = value
                continue
            row = 0
            for start, size in parts:
                for i in range(size // TILE):
                    s = (start - BASE[level]) // (TILE * PER[level]) + i // PER[level]
                    rho = offs[level] + (1 << level) * (i % PER[level])
                    at = tile_at(s * ROWS + rho * TILE)
                    acc[which, at] = acc[which, at] + value[row : row + TILE]
                    row += TILE
    for s in range(8):
        at = tile_at(s * ROWS + offs[3] * TILE)
        part = slice(s * TILE, (s + 1) * TILE)
        for which in range(3):
            total = acc[which, at] + acc3[which, part]
            acc[which, at] = total
            if which > 0:
                own3[which - 1, part] = total
    for s, (dz, dc) in enumerate(SLOTS):
        home = core.at[dz] if dc else (zs[dz - 1].at[0] if dz else own)
        home[0] = att[s]
        for which in range(3):
            home[1 + which] = acc[which, s * ROWS : (s + 1) * ROWS].astype(BF16)


MSGS = [shape(BF16, 4, ROWS, HD)] + [shape(BF16, 2, 4, ROWS, HD)] * 3
CORES = shape(BF16, 4, 4, ROWS, HD)


def backward(info, comp, p, do, c, acc3, att):
    return call(
        bwd_kernel,
        MSGS + [CORES, shape(F32, 2, ROWS, HD)],
        [SM] + [VM] * 6,
        [VM] * 6,
        [pltpu.VMEM((3, 1024, HD), F32)],
        cost=pl.CostEstimate(flops=600000000, bytes_accessed=6000000, transcendentals=0),
    )(info, comp, p, do, c, acc3, att)


def full(*dims):
    return pl.BlockSpec(dims, lambda i, info: (0,) * len(dims))


def patch(kernel, outs, blocks, ins, in_blocks, info):
    count = len(blocks)
    return pl.pallas_call(
        kernel,
        out_shape=outs,
        grid_spec=pltpu.PrefetchScalarGridSpec(
            num_scalar_prefetch=1,
            grid=(1,),
            in_specs=[pl.BlockSpec(memory_space=pl.ANY)] * count + in_blocks,
            out_specs=blocks + [full(*x.shape) for x in outs[count:]],
        ),
        input_output_aliases={1 + n: n for n in range(count)},
        compiler_params=PARAMS,
    )(info, *ins)


def merge_kernel(info, *refs):
    own3, xin, bias = refs[5:8]
    own, zs, core, bias_out = refs[8], refs[9:12], refs[12], refs[13]
    terms = jnp.sum(xin[2 * ROWS :].astype(F32), axis=0, keepdims=True)
    bias_out[...] = bias[...] + terms
    for s, (dz, dc) in enumerate(SLOTS):
        at = slice(s * TILE, (s + 1) * TILE)
        for a in range(2):
            theirs = xin[a * ROWS + s * TILE : a * ROWS + (s + 1) * TILE]
            total = (own3[a, at] + theirs.astype(F32)).astype(BF16)
            if dc:
                core[dz, a] = total
            elif dz:
                zs[dz - 1][0, a] = total
            else:
                own[a] = total


def merge(info, msgs, own3, xin, bias):
    one = pl.BlockSpec((2, TILE, HD), lambda i, info: (1, info[3], 0))
    two = pl.BlockSpec((1, 2, TILE, HD), lambda i, info: (0, 1, info[3], 0))
    four = pl.BlockSpec((4, 2, TILE, HD), lambda i, info: (0, 1, info[3], 0))
    return patch(
        merge_kernel,
        MSGS + [CORES, shape(F32, 1, 128)],
        [one, two, two, two, four],
        [*msgs, own3, xin, bias],
        [full(2, ROWS, HD), full(2 * ROWS + TILE, HD), full(1, 128)],
        info,
    )


def relay_kernel(info, *refs):
    core, bias, theirs = refs[3:6]
    zs, spread = refs[6:9], refs[9]
    for dz in range(1, 4):
        zs[dz - 1][0] = core[4 - dz]
    spread[...] = jnp.broadcast_to((bias[...] + theirs[...])[:, : LEVELS * H], spread.shape)


def relay(info, msgs, core, biases, devices):
    half = pl.BlockSpec((1, 4, ROWS, HD), lambda i, info: (1, 0, 0, 0))
    return patch(
        relay_kernel,
        MSGS[1:] + [shape(F32, devices, LEVELS * H)],
        [half] * 3,
        [*msgs, core, *biases],
        [full(*CORES.shape), full(1, 128), full(1, 128)],
        info,
    )


def unpack_kernel(info, *refs):
    own, core = refs[0], refs[4]
    zs = [refs[2], refs[1], refs[3]]
    outs = refs[5:9]
    e = info[4]
    order = row_order(True)
    for a in range(4):
        for dz, dc in SLOTS:
            home = zs[3 - dz if dc else dz - 1].at[dc] if dz else (core.at[0] if dc else own)
            at = head_at(dest_head(e, dz, dc))
            outs[a][:, at] = dot_nn(order, home[a]).astype(BF16)


def total_kernel(bias, out):
    total = jnp.sum(bias[...], axis=0, keepdims=True)
    for level in range(LEVELS):
        out[level : level + 1] = total[:, level * H : (level + 1) * H]


def bias_total(bias):
    return call(total_kernel, shape(F32, LEVELS, H), [VM], VM)(bias)


def unpack(info, own, zs, core):
    return call(
        unpack_kernel,
        [shape(BF16, ROWS, H * HD)] * 4,
        [SM] + [VM] * 5,
        [VM] * 4,
        cost=SHADOW,
    )(info, own, zs[1], zs[0], zs[2], core)


def local(queries, keys, values, cotangent, head_offsets, level_bias):
    def move(x, pairs):
        return lax.ppermute(x, "seq", pairs)

    packed = pack(head_offsets, keys, values, queries, cotangent)
    sent, info = packed[:8], packed[8]
    got = [sent[0]] + [None] * 7
    for slot in SEND:
        got[slot] = move(sent[slot], z_perm(*SLOTS[slot]))
    xkv = move(pick3(info, got), xor_perm(8))
    comp, p, o, z = forward(info, got)
    att, do, c, acc3, xout, bias = mixing(info, level_bias, comp, o, z, xkv)
    xin = move(xout, xor_perm(8))
    *msgs, own3 = backward(info, comp, p, do, c, acc3, att)
    own, *zs, core, bias = merge(info, msgs, own3, xin, bias)
    core = move(core, xor_perm(1))
    biases = [bias, move(bias, xor_perm(1))]
    *zs, spread = relay(info, zs, core, biases, 64)
    zs = [move(x, back_perm(dz, 0)) for dz, x in zip((1, 2, 3), zs)]
    bias = lax.all_to_all(
        spread, ("grp", "seq"), 0, 0, axis_index_groups=GROUPS, tiled=True
    )
    outs = unpack(info, own, zs, core)
    outs, bias = lax.optimization_barrier((outs, bias))
    return (*outs, bias_total(bias))


def solution(mesh):
    rows = P(("grp", "seq"), None)
    return jax.shard_map(
        local,
        mesh=mesh,
        in_specs=(rows, rows, rows, rows, P(), P()),
        out_specs=(rows, rows, rows, rows, P()),
        check_vma=False,
    )
```

```python
import jax
import jax.numpy as jnp
from jax import lax
from jax.experimental import pallas as pl
from jax.experimental.pallas import tpu as pltpu
from jax.sharding import PartitionSpec as P

H = 8
HD = 128
LEVELS = 4
ROWS = 128
TILE = 16
SHADOW = pl.CostEstimate(flops=0, bytes_accessed=200000000, transcendentals=0)
BIG = 53 * 1024 * 1024
RES = 8
SCALE = HD ** (-0.5)
F32 = jnp.float32
BF16 = jnp.bfloat16
I32 = jnp.int32
VM = pl.BlockSpec(memory_space=pltpu.VMEM)
SM = pl.BlockSpec(memory_space=pltpu.SMEM)
PARAMS = pltpu.CompilerParams(vmem_limit_bytes=16 * 1024 * 1024)

SLOTS = [(dz, dc) for dz in range(4) for dc in range(2)]
CORE, FAR, FAR2 = 1, 4, 5
NEAR = [2, 6, 3, 7]
SEND = [CORE] + NEAR + [FAR, FAR2]

PER = [8, 4, 2, 1]
BASE = [0, 1024, 1536, 1792]
COMPACT = 1920


GROUPS = [
    [g * 32 + i for g in range(8) for i in range(32) if (i // 8 % 2, i % 2) == (n, core)]
    for n in range(2)
    for core in range(2)
]


def z_perm(dz, dc):
    pairs = []
    for i in range(32):
        x, z, c = i // 8, i % 8 // 2, i % 2
        step = -dz if c ^ dc else dz
        pairs.append((i, x * 8 + (z + step) % 4 * 2 + (c ^ dc)))
    return pairs


def back_perm(dz, dc):
    return [(b, a) for a, b in z_perm(dz, dc)]


def xor_perm(bits):
    return [(i, i ^ bits) for i in range(32)]


def dest_head(e, dz, dc):
    z = e // 2
    c = e - 2 * z
    cd = c if dc == 0 else 1 - c
    return lax.rem(z + dz + cd * (4 - 2 * dz), 4) * 2 + cd


def dot_nn(a, b):
    return jnp.dot(a, b, preferred_element_type=F32)


def dot_nt(a, b):
    return lax.dot_general(a, b, (((1,), (1,)), ((), ())), preferred_element_type=F32)


def dot_tn(a, b):
    return lax.dot_general(a, b, (((0,), (0,)), ((), ())), preferred_element_type=F32)


def row_order(transposed):
    shape = (ROWS, ROWS)
    packed = lax.broadcasted_iota(I32, shape, 1 if transposed else 0)
    plain = lax.broadcasted_iota(I32, shape, 0 if transposed else 1)
    return (plain == (packed % TILE) * RES + packed // TILE).astype(BF16)


def tile_at(row):
    return pl.ds(pl.multiple_of(row, TILE), TILE)


def head_at(h):
    return pl.ds(pl.multiple_of(h * HD, HD), HD)


def shape(dtype, *dims):
    return jax.ShapeDtypeStruct(dims, dtype)


def call(kernel, outs, ins, out_specs, scratch=(), cost=None):
    return pl.pallas_call(
        kernel,
        out_shape=outs,
        in_specs=ins,
        out_specs=out_specs,
        scratch_shapes=list(scratch),
        compiler_params=PARAMS,
        cost_estimate=cost,
    )


def pack_kernel(offs, k, v, q, d, *rest):
    outs, info, tmp = rest[:8], rest[8], rest[9]
    e = lax.rem(lax.axis_index("seq"), 8)
    order = row_order(False)
    for level in range(LEVELS):
        info[level] = offs[level, e]
    info[4] = e
    info[5] = dest_head(e, 2, 0) // 2
    for a, ref in enumerate((k, v, q, d)):
        tmp[...] = dot_nn(order, ref[...]).astype(BF16)
        for slot, (dz, dc) in enumerate(SLOTS):
            outs[slot][a] = tmp[:, head_at(dest_head(e, dz, dc))]


def pack(offs, k, v, q, d):
    return pl.pallas_call(
        pack_kernel,
        out_shape=[shape(BF16, 4, ROWS, HD)] * 8 + [shape(I32, 8)],
        in_specs=[SM] + [VM] * 4,
        out_specs=[VM] * 8 + [SM],
        scratch_shapes=[pltpu.VMEM((ROWS, H * HD), BF16)],
        compiler_params=pltpu.CompilerParams(vmem_limit_bytes=BIG),
    )(offs, k, v, q, d)


def by_slot(refs):
    return [refs[([0] + SEND).index(slot)] for slot in range(8)]


def in_order(got):
    return [got[slot] for slot in [0] + SEND]


def pick_kernel(info, *refs):
    got, out = by_slot(refs[:8]), refs[8]
    rows = tile_at(info[3] * TILE)
    for s in range(8):
        out[:, s * TILE : (s + 1) * TILE] = got[s][0:2, rows]


def pick3(info, got):
    return call(pick_kernel, shape(BF16, 2, ROWS, HD), [SM] + [VM] * 8, VM)(
        info, *in_order(got)
    )


def join(pieces):
    return pieces[0] if len(pieces) == 1 else jnp.concatenate(pieces, axis=0)


def load(ref, parts):
    return join([ref[pl.ds(start, size)] for start, size in parts])


def store(ref, parts, value):
    row = 0
    for start, size in parts:
        ref[pl.ds(start, size)] = value[row : row + size]
        row += size


def segments(e):
    mate = jnp.where(lax.rem(e // 2 + e, 2) == 0, 3, 1)
    near = pl.multiple_of(BASE[1] + mate * 128, 128)
    far = pl.multiple_of(BASE[1] + (4 - mate) * 128, 128)
    segs = [(0, [(m * 256, 256)]) for m in range(4)]
    segs.append((1, [(BASE[1], 128), (near, 128)]))
    segs.append((1, [(BASE[1] + 256, 128), (far, 128)]))
    segs.append((2, [(BASE[2], 256)]))
    return segs


def kept(level, off):
    r = 1 << level
    return [s * ROWS + (off + r * t) * TILE for s in range(8) for t in range(PER[level])]


def wide(column):
    return jnp.broadcast_to(column, (column.shape[0], HD))


def twice(x):
    return jnp.concatenate([x, x], axis=1)


def row_sum(x):
    return wide(jnp.sum(x, axis=-1, keepdims=True))


def softmax_rows(q, k, v):
    s = dot_nt(q, k) * SCALE
    m = jnp.max(s, axis=-1, keepdims=True)
    p = jnp.exp(s - m)
    l = jnp.sum(p, axis=-1, keepdims=True)
    p = p * (1.0 / l)
    return p, wide(m + jnp.log(l)), dot_nn(p.astype(BF16), v)


def fwd_kernel(info, *refs):
    got = by_slot(refs[:8])
    comp, p_s, o_s, z_s = refs[8:]
    for a in range(4):
        for s in range(8):
            comp[a, s * ROWS : (s + 1) * ROWS] = got[s][a]
            for level in range(1, LEVELS):
                for t in range(PER[level]):
                    at = tile_at((info[level] + (1 << level) * t) * TILE)
                    row = BASE[level] + (s * PER[level] + t) * TILE
                    comp[a, row : row + TILE] = got[s][a, at]
    for level, parts in segments(info[4]):
        q, k, v = (load(comp.at[a], parts) for a in (2, 0, 1))
        p, lse, o = softmax_rows(q, k, v)
        store(p_s, parts, p)
        store(z_s, parts, lse)
        store(o_s, parts, o)


def forward(info, got):
    return call(
        fwd_kernel,
        [
            shape(BF16, 4, COMPACT, HD),
            shape(F32, BASE[3], 256),
            shape(F32, BASE[3], HD),
            shape(F32, BASE[3], HD),
        ],
        [SM] + [VM] * 8,
        [VM] * 4,
        cost=pl.CostEstimate(flops=250000000, bytes_accessed=6000000, transcendentals=460000),
    )(info, *in_order(got))


def mix_kernel(info, bias, comp, o_s, z_s, xkv, *refs):
    att, do_s, c_s, acc3, xout, bias_out, z_t, lz_s, d_s = refs
    e = info[4]
    offs = [info[level] for level in range(LEVELS)]
    last = slice(BASE[3], COMPACT)
    q3 = comp[2, last]
    k3 = jnp.concatenate([comp[0, last], xkv[0]], axis=0)
    v3 = jnp.concatenate([comp[1, last], xkv[1]], axis=0)
    p3, lse3, o3 = softmax_rows(q3, k3, v3)
    for level in range(LEVELS - 1):
        at = slice(BASE[level], BASE[level + 1])
        z_t[at] = z_s[at] + bias[level, e]
    z_t[last] = lse3 + bias[3, e]

    ninf = jnp.float32(-jnp.inf)
    for s in range(8):
        rows = slice(s * ROWS, (s + 1) * ROWS)
        zs = [z_t[rows]]
        os = [o_s[rows]]
        for level in range(1, LEVELS):
            r = 1 << level
            zp, op = [], []
            for rho in range(RES):
                row = BASE[level] + (s * PER[level] + rho // r) * TILE
                zp.append(jnp.where(offs[level] == rho % r, z_t[row : row + TILE], ninf))
                if level == 3:
                    op.append(o3[s * TILE : (s + 1) * TILE])
                else:
                    op.append(o_s[row : row + TILE])
            zs.append(join(zp))
            os.append(join(op))
        top = jnp.maximum(jnp.maximum(zs[0], zs[1]), jnp.maximum(zs[2], zs[3]))
        es = [jnp.exp(x - top) for x in zs]
        den = es[0] + es[1] + es[2] + es[3]
        inv = 1.0 / den
        out = (es[0] * inv) * os[0]
        for level in range(1, LEVELS):
            out = out + (es[level] * inv) * os[level]
        att[s] = out.astype(BF16)
        lz_s[rows] = top + jnp.log(den)
        d_s[rows] = row_sum(comp[3, rows].astype(F32) * out)

    lane = lax.broadcasted_iota(I32, (1, 128), 1)
    biases = jnp.zeros((1, 128), F32)
    for level in (3, 0, 1, 2):
        end = COMPACT if level == 3 else BASE[level + 1]
        span = slice(BASE[level], end)
        if level == 0:
            lz, dd = lz_s[span], d_s[span]
        else:
            places = kept(level, offs[level])
            lz = join([lz_s[tile_at(x)] for x in places])
            dd = join([d_s[tile_at(x)] for x in places])
        cot = comp[3, span].astype(F32)
        o = o3 if level == 3 else o_s[span]
        a = jnp.exp(z_t[span] - lz)
        do = (a * cot).astype(BF16)
        g = a * (row_sum(cot * o) - dd)
        c = row_sum(do.astype(F32) * o) - g
        total = jnp.sum(g, axis=0, keepdims=True)
        biases = biases + jnp.where(lane == level * H + e, total, 0.0)
        if level < 3:
            do_s[span] = do
            c_s[span] = c
            continue
        dp = dot_nt(do, v3)
        ds = (p3 * (dp - twice(c))).astype(BF16)
        acc3[0] = dot_nn(ds, k3) * SCALE
        both = dot_tn(
            jnp.concatenate([ds, p3.astype(BF16)], axis=1),
            jnp.concatenate([q3, do], axis=1),
        )
        for n, value in ((1, both[:256, :HD] * SCALE), (2, both[256:, HD:])):
            acc3[n] = value[:ROWS]
            xout[(n - 1) * ROWS : n * ROWS] = value[ROWS:].astype(BF16)
    bias_out[...] = biases
    high = biases.astype(BF16).astype(F32)
    middle = (biases - high).astype(BF16).astype(F32)
    row = lax.broadcasted_iota(I32, (TILE, 128), 0)
    terms = jnp.where(row == 0, high, jnp.where(row == 1, middle, biases - high - middle))
    xout[2 * ROWS :] = jnp.where(row < 3, terms, 0.0).astype(BF16)


def mixing(info, bias, comp, o, z, xkv):
    return call(
        mix_kernel,
        [
            shape(BF16, 8, ROWS, HD),
            shape(BF16, BASE[3], HD),
            shape(F32, BASE[3], HD),
            shape(F32, 3, ROWS, HD),
            shape(BF16, 2 * ROWS + TILE, HD),
            shape(F32, 1, 128),
        ],
        [SM, SM] + [VM] * 4,
        [VM] * 6,
        [
            pltpu.VMEM((COMPACT, HD), F32),
            pltpu.VMEM((1024, HD), F32),
            pltpu.VMEM((1024, HD), F32),
        ],
        cost=pl.CostEstimate(flops=50000000, bytes_accessed=6000000, transcendentals=40000),
    )(info, bias, comp, o, z, xkv)


def bwd_kernel(info, comp, p_s, do_s, c_s, acc3, att, *refs):
    own, zs, core, own3, acc = refs[0], refs[1:4], refs[4], refs[5], refs[6]
    offs = [info[level] for level in range(LEVELS)]
    for level, parts in segments(info[4]):
        q, k, v = (load(comp.at[a], parts) for a in (2, 0, 1))
        p, do = load(p_s, parts), load(do_s, parts)
        ds = (p * (dot_nt(do, v) - twice(load(c_s, parts)))).astype(BF16)
        dq = dot_nn(ds, k) * SCALE
        both = dot_tn(
            jnp.concatenate([ds, p.astype(BF16)], axis=1),
            jnp.concatenate([q, do], axis=1),
        )
        dk = both[:256, :HD] * SCALE
        dv = both[256:, HD:]
        for which, value in enumerate((dq, dk, dv)):
            if level == 0:
                acc[which, pl.ds(parts[0][0], 256)] = value
                continue
            row = 0
            for start, size in parts:
                for i in range(size // TILE):
                    s = (start - BASE[level]) // (TILE * PER[level]) + i // PER[level]
                    rho = offs[level] + (1 << level) * (i % PER[level])
                    at = tile_at(s * ROWS + rho * TILE)
                    acc[which, at] = acc[which, at] + value[row : row + TILE]
                    row += TILE
    for s in range(8):
        at = tile_at(s * ROWS + offs[3] * TILE)
        part = slice(s * TILE, (s + 1) * TILE)
        for which in range(3):
            total = acc[which, at] + acc3[which, part]
            acc[which, at] = total
            if which > 0:
                own3[which - 1, part] = total
    for s, (dz, dc) in enumerate(SLOTS):
        home = core.at[dz] if dc else (zs[dz - 1].at[0] if dz else own)
        home[0] = att[s]
        for which in range(3):
            home[1 + which] = acc[which, s * ROWS : (s + 1) * ROWS].astype(BF16)


MSGS = [shape(BF16, 4, ROWS, HD)] + [shape(BF16, 2, 4, ROWS, HD)] * 3
CORES = shape(BF16, 4, 4, ROWS, HD)


def backward(info, comp, p, do, c, acc3, att):
    return call(
        bwd_kernel,
        MSGS + [CORES, shape(F32, 2, ROWS, HD)],
        [SM] + [VM] * 6,
        [VM] * 6,
        [pltpu.VMEM((3, 1024, HD), F32)],
        cost=pl.CostEstimate(flops=600000000, bytes_accessed=6000000, transcendentals=0),
    )(info, comp, p, do, c, acc3, att)


def full(*dims):
    return pl.BlockSpec(dims, lambda i, info: (0,) * len(dims))


def patch(kernel, outs, blocks, ins, in_blocks, info):
    count = len(blocks)
    return pl.pallas_call(
        kernel,
        out_shape=outs,
        grid_spec=pltpu.PrefetchScalarGridSpec(
            num_scalar_prefetch=1,
            grid=(1,),
            in_specs=[pl.BlockSpec(memory_space=pl.ANY)] * count + in_blocks,
            out_specs=blocks + [full(*x.shape) for x in outs[count:]],
        ),
        input_output_aliases={1 + n: n for n in range(count)},
        compiler_params=PARAMS,
    )(info, *ins)


def merge_kernel(info, *refs):
    own3, xin, bias = refs[5:8]
    own, zs, core, bias_out = refs[8], refs[9:12], refs[12], refs[13]
    terms = jnp.sum(xin[2 * ROWS :].astype(F32), axis=0, keepdims=True)
    bias_out[...] = bias[...] + terms
    for s, (dz, dc) in enumerate(SLOTS):
        at = slice(s * TILE, (s + 1) * TILE)
        for a in range(2):
            theirs = xin[a * ROWS + s * TILE : a * ROWS + (s + 1) * TILE]
            total = (own3[a, at] + theirs.astype(F32)).astype(BF16)
            if dc:
                core[dz, a] = total
            elif dz:
                zs[dz - 1][0, a] = total
            else:
                own[a] = total


def merge(info, msgs, own3, xin, bias):
    one = pl.BlockSpec((2, TILE, HD), lambda i, info: (1, info[3], 0))
    two = pl.BlockSpec((1, 2, TILE, HD), lambda i, info: (0, 1, info[3], 0))
    four = pl.BlockSpec((4, 2, TILE, HD), lambda i, info: (0, 1, info[3], 0))
    return patch(
        merge_kernel,
        MSGS + [CORES, shape(F32, 1, 128)],
        [one, two, two, two, four],
        [*msgs, own3, xin, bias],
        [full(2, ROWS, HD), full(2 * ROWS + TILE, HD), full(1, 128)],
        info,
    )


def relay_kernel(info, *refs):
    core, bias, theirs = refs[3:6]
    zs, total = refs[6:9], refs[9]
    for dz in range(1, 4):
        zs[dz - 1][0] = core[4 - dz]
    total[...] = bias[...] + theirs[...]


def relay(info, msgs, core, biases):
    half = pl.BlockSpec((1, 4, ROWS, HD), lambda i, info: (1, 0, 0, 0))
    return patch(
        relay_kernel,
        MSGS[1:] + [shape(F32, 1, 128)],
        [half] * 3,
        [*msgs, core, *biases],
        [full(*CORES.shape), full(1, 128), full(1, 128)],
        info,
    )


def unpack_kernel(info, *refs):
    own, core = refs[0], refs[4]
    zs = [refs[2], refs[1], refs[3]]
    outs = refs[5:9]
    e = info[4]
    order = row_order(True)
    for a in range(4):
        for dz, dc in SLOTS:
            home = zs[3 - dz if dc else dz - 1].at[dc] if dz else (core.at[0] if dc else own)
            at = head_at(dest_head(e, dz, dc))
            outs[a][:, at] = dot_nn(order, home[a]).astype(BF16)


def total_kernel(bias, out):
    total = jnp.sum(bias[...], axis=0, keepdims=True)
    for level in range(LEVELS):
        out[level : level + 1] = total[:, level * H : (level + 1) * H]


def bias_total(bias):
    return call(total_kernel, shape(F32, LEVELS, H), [VM], VM)(bias)


def unpack(info, own, zs, core):
    return call(
        unpack_kernel,
        [shape(BF16, ROWS, H * HD)] * 4,
        [SM] + [VM] * 5,
        [VM] * 4,
        cost=SHADOW,
    )(info, own, zs[1], zs[0], zs[2], core)


def local(queries, keys, values, cotangent, head_offsets, level_bias):
    def move(x, pairs):
        return lax.ppermute(x, "seq", pairs)

    packed = pack(head_offsets, keys, values, queries, cotangent)
    sent, info = packed[:8], packed[8]
    got = [sent[0]] + [None] * 7
    for slot in SEND:
        got[slot] = move(sent[slot], z_perm(*SLOTS[slot]))
    xkv = move(pick3(info, got), xor_perm(8))
    comp, p, o, z = forward(info, got)
    att, do, c, acc3, xout, bias = mixing(info, level_bias, comp, o, z, xkv)
    xin = move(xout, xor_perm(8))
    *msgs, own3 = backward(info, comp, p, do, c, acc3, att)
    own, *zs, core, bias = merge(info, msgs, own3, xin, bias)
    core = move(core, xor_perm(1))
    biases = [bias, move(bias, xor_perm(1))]
    *zs, bias = relay(info, zs, core, biases)
    zs = [move(x, back_perm(dz, 0)) for dz, x in zip((1, 2, 3), zs)]
    spread = jnp.broadcast_to(bias[:, : LEVELS * H], (64, LEVELS * H))
    bias = lax.all_to_all(
        spread, ("grp", "seq"), 0, 0, axis_index_groups=GROUPS, tiled=True
    )
    outs = unpack(info, own, zs, core)
    outs, bias = lax.optimization_barrier((outs, bias))
    return (*outs, bias_total(bias))


def solution(mesh):
    rows = P(("grp", "seq"), None)
    return jax.shard_map(
        local,
        mesh=mesh,
        in_specs=(rows, rows, rows, rows, P(), P()),
        out_specs=(rows, rows, rows, rows, P()),
        check_vma=False,
    )
```

```python
import jax
import jax.numpy as jnp
from jax import lax
from jax.experimental import pallas as pl
from jax.experimental.pallas import tpu as pltpu
from jax.sharding import PartitionSpec as P

H = 8
HD = 128
LEVELS = 4
ROWS = 128
TILE = 16
SHADOW = pl.CostEstimate(flops=0, bytes_accessed=200000000, transcendentals=0)
BIG = 54144 * 1024
RES = 8
SCALE = HD ** (-0.5)
F32 = jnp.float32
BF16 = jnp.bfloat16
I32 = jnp.int32
VM = pl.BlockSpec(memory_space=pltpu.VMEM)
SM = pl.BlockSpec(memory_space=pltpu.SMEM)
PARAMS = pltpu.CompilerParams(vmem_limit_bytes=16 * 1024 * 1024)

SLOTS = [(dz, dc) for dz in range(4) for dc in range(2)]
CORE, FAR, FAR2 = 1, 4, 5
NEAR = [2, 6, 3, 7]
SEND = [CORE] + NEAR + [FAR, FAR2]

PER = [8, 4, 2, 1]
BASE = [0, 1024, 1536, 1792]
COMPACT = 1920


GROUPS = [
    [g * 32 + i for g in range(8) for i in range(32) if (i // 8 % 2, i % 2) == (n, core)]
    for n in range(2)
    for core in range(2)
]


def z_perm(dz, dc):
    pairs = []
    for i in range(32):
        x, z, c = i // 8, i % 8 // 2, i % 2
        step = -dz if c ^ dc else dz
        pairs.append((i, x * 8 + (z + step) % 4 * 2 + (c ^ dc)))
    return pairs


def back_perm(dz, dc):
    return [(b, a) for a, b in z_perm(dz, dc)]


def xor_perm(bits):
    return [(i, i ^ bits) for i in range(32)]


def dest_head(e, dz, dc):
    z = e // 2
    c = e - 2 * z
    cd = c if dc == 0 else 1 - c
    return lax.rem(z + dz + cd * (4 - 2 * dz), 4) * 2 + cd


def dot_nn(a, b):
    return jnp.dot(a, b, preferred_element_type=F32)


def dot_nt(a, b):
    return lax.dot_general(a, b, (((1,), (1,)), ((), ())), preferred_element_type=F32)


def dot_tn(a, b):
    return lax.dot_general(a, b, (((0,), (0,)), ((), ())), preferred_element_type=F32)


def row_order(transposed):
    shape = (ROWS, ROWS)
    packed = lax.broadcasted_iota(I32, shape, 1 if transposed else 0)
    plain = lax.broadcasted_iota(I32, shape, 0 if transposed else 1)
    return (plain == (packed % TILE) * RES + packed // TILE).astype(BF16)


def tile_at(row):
    return pl.ds(pl.multiple_of(row, TILE), TILE)


def head_at(h):
    return pl.ds(pl.multiple_of(h * HD, HD), HD)


def shape(dtype, *dims):
    return jax.ShapeDtypeStruct(dims, dtype)


def call(kernel, outs, ins, out_specs, scratch=(), cost=None):
    return pl.pallas_call(
        kernel,
        out_shape=outs,
        in_specs=ins,
        out_specs=out_specs,
        scratch_shapes=list(scratch),
        compiler_params=PARAMS,
        cost_estimate=cost,
    )


def pack_kernel(offs, k, v, q, d, *rest):
    outs, info, tmp = rest[:8], rest[8], rest[9]
    e = lax.rem(lax.axis_index("seq"), 8)
    order = row_order(False)
    for level in range(LEVELS):
        info[level] = offs[level, e]
    info[4] = e
    info[5] = dest_head(e, 2, 0) // 2
    for a, ref in enumerate((k, v, q, d)):
        tmp[...] = dot_nn(order, ref[...]).astype(BF16)
        for slot, (dz, dc) in enumerate(SLOTS):
            outs[slot][a] = tmp[:, head_at(dest_head(e, dz, dc))]


def pack(offs, k, v, q, d):
    return pl.pallas_call(
        pack_kernel,
        out_shape=[shape(BF16, 4, ROWS, HD)] * 8 + [shape(I32, 8)],
        in_specs=[SM] + [VM] * 4,
        out_specs=[VM] * 8 + [SM],
        scratch_shapes=[pltpu.VMEM((ROWS, H * HD), BF16)],
        compiler_params=pltpu.CompilerParams(vmem_limit_bytes=BIG),
    )(offs, k, v, q, d)


def by_slot(refs):
    return [refs[([0] + SEND).index(slot)] for slot in range(8)]


def in_order(got):
    return [got[slot] for slot in [0] + SEND]


def pick_kernel(info, *refs):
    got, out = by_slot(refs[:8]), refs[8]
    rows = tile_at(info[3] * TILE)
    for s in range(8):
        out[:, s * TILE : (s + 1) * TILE] = got[s][0:2, rows]


def pick3(info, got):
    return call(pick_kernel, shape(BF16, 2, ROWS, HD), [SM] + [VM] * 8, VM)(
        info, *in_order(got)
    )


def join(pieces):
    return pieces[0] if len(pieces) == 1 else jnp.concatenate(pieces, axis=0)


def load(ref, parts):
    return join([ref[pl.ds(start, size)] for start, size in parts])


def store(ref, parts, value):
    row = 0
    for start, size in parts:
        ref[pl.ds(start, size)] = value[row : row + size]
        row += size


def segments(e):
    mate = jnp.where(lax.rem(e // 2 + e, 2) == 0, 3, 1)
    near = pl.multiple_of(BASE[1] + mate * 128, 128)
    far = pl.multiple_of(BASE[1] + (4 - mate) * 128, 128)
    segs = [(0, [(m * 256, 256)]) for m in range(4)]
    segs.append((1, [(BASE[1], 128), (near, 128)]))
    segs.append((1, [(BASE[1] + 256, 128), (far, 128)]))
    segs.append((2, [(BASE[2], 256)]))
    return segs


def kept(level, off):
    r = 1 << level
    return [s * ROWS + (off + r * t) * TILE for s in range(8) for t in range(PER[level])]


def wide(column):
    return jnp.broadcast_to(column, (column.shape[0], HD))


def twice(x):
    return jnp.concatenate([x, x], axis=1)


def row_sum(x):
    return wide(jnp.sum(x, axis=-1, keepdims=True))


def softmax_rows(q, k, v):
    s = dot_nt(q, k) * SCALE
    m = jnp.max(s, axis=-1, keepdims=True)
    p = jnp.exp(s - m)
    l = jnp.sum(p, axis=-1, keepdims=True)
    p = p * (1.0 / l)
    return p, wide(m + jnp.log(l)), dot_nn(p.astype(BF16), v)


def fwd_kernel(info, *refs):
    got = by_slot(refs[:8])
    comp, p_s, o_s, z_s = refs[8:]
    for a in range(4):
        for s in range(8):
            comp[a, s * ROWS : (s + 1) * ROWS] = got[s][a]
            for level in range(1, LEVELS):
                for t in range(PER[level]):
                    at = tile_at((info[level] + (1 << level) * t) * TILE)
                    row = BASE[level] + (s * PER[level] + t) * TILE
                    comp[a, row : row + TILE] = got[s][a, at]
    for level, parts in segments(info[4]):
        q, k, v = (load(comp.at[a], parts) for a in (2, 0, 1))
        p, lse, o = softmax_rows(q, k, v)
        store(p_s, parts, p)
        store(z_s, parts, lse)
        store(o_s, parts, o)


def forward(info, got):
    return call(
        fwd_kernel,
        [
            shape(BF16, 4, COMPACT, HD),
            shape(F32, BASE[3], 256),
            shape(F32, BASE[3], HD),
            shape(F32, BASE[3], HD),
        ],
        [SM] + [VM] * 8,
        [VM] * 4,
        cost=pl.CostEstimate(flops=250000000, bytes_accessed=6000000, transcendentals=460000),
    )(info, *in_order(got))


def mix_kernel(info, bias, comp, o_s, z_s, xkv, *refs):
    att, do_s, c_s, acc3, xout, bias_out, z_t, lz_s, d_s = refs
    e = info[4]
    offs = [info[level] for level in range(LEVELS)]
    last = slice(BASE[3], COMPACT)
    q3 = comp[2, last]
    k3 = jnp.concatenate([comp[0, last], xkv[0]], axis=0)
    v3 = jnp.concatenate([comp[1, last], xkv[1]], axis=0)
    p3, lse3, o3 = softmax_rows(q3, k3, v3)
    for level in range(LEVELS - 1):
        at = slice(BASE[level], BASE[level + 1])
        z_t[at] = z_s[at] + bias[level, e]
    z_t[last] = lse3 + bias[3, e]

    ninf = jnp.float32(-jnp.inf)
    for s in range(8):
        rows = slice(s * ROWS, (s + 1) * ROWS)
        zs = [z_t[rows]]
        os = [o_s[rows]]
        for level in range(1, LEVELS):
            r = 1 << level
            zp, op = [], []
            for rho in range(RES):
                row = BASE[level] + (s * PER[level] + rho // r) * TILE
                zp.append(jnp.where(offs[level] == rho % r, z_t[row : row + TILE], ninf))
                if level == 3:
                    op.append(o3[s * TILE : (s + 1) * TILE])
                else:
                    op.append(o_s[row : row + TILE])
            zs.append(join(zp))
            os.append(join(op))
        top = jnp.maximum(jnp.maximum(zs[0], zs[1]), jnp.maximum(zs[2], zs[3]))
        es = [jnp.exp(x - top) for x in zs]
        den = es[0] + es[1] + es[2] + es[3]
        inv = 1.0 / den
        out = (es[0] * inv) * os[0]
        for level in range(1, LEVELS):
            out = out + (es[level] * inv) * os[level]
        att[s] = out.astype(BF16)
        lz_s[rows] = top + jnp.log(den)
        d_s[rows] = row_sum(comp[3, rows].astype(F32) * out)

    lane = lax.broadcasted_iota(I32, (1, 128), 1)
    biases = jnp.zeros((1, 128), F32)
    for level in (3, 0, 1, 2):
        end = COMPACT if level == 3 else BASE[level + 1]
        span = slice(BASE[level], end)
        if level == 0:
            lz, dd = lz_s[span], d_s[span]
        else:
            places = kept(level, offs[level])
            lz = join([lz_s[tile_at(x)] for x in places])
            dd = join([d_s[tile_at(x)] for x in places])
        cot = comp[3, span].astype(F32)
        o = o3 if level == 3 else o_s[span]
        a = jnp.exp(z_t[span] - lz)
        do = (a * cot).astype(BF16)
        g = a * (row_sum(cot * o) - dd)
        c = row_sum(do.astype(F32) * o) - g
        total = jnp.sum(g, axis=0, keepdims=True)
        biases = biases + jnp.where(lane == level * H + e, total, 0.0)
        if level < 3:
            do_s[span] = do
            c_s[span] = c
            continue
        dp = dot_nt(do, v3)
        ds = (p3 * (dp - twice(c))).astype(BF16)
        acc3[0] = dot_nn(ds, k3) * SCALE
        both = dot_tn(
            jnp.concatenate([ds, p3.astype(BF16)], axis=1),
            jnp.concatenate([q3, do], axis=1),
        )
        for n, value in ((1, both[:256, :HD] * SCALE), (2, both[256:, HD:])):
            acc3[n] = value[:ROWS]
            xout[(n - 1) * ROWS : n * ROWS] = value[ROWS:].astype(BF16)
    bias_out[...] = biases
    high = biases.astype(BF16).astype(F32)
    middle = (biases - high).astype(BF16).astype(F32)
    row = lax.broadcasted_iota(I32, (TILE, 128), 0)
    terms = jnp.where(row == 0, high, jnp.where(row == 1, middle, biases - high - middle))
    xout[2 * ROWS :] = jnp.where(row < 3, terms, 0.0).astype(BF16)


def mixing(info, bias, comp, o, z, xkv):
    return call(
        mix_kernel,
        [
            shape(BF16, 8, ROWS, HD),
            shape(BF16, BASE[3], HD),
            shape(F32, BASE[3], HD),
            shape(F32, 3, ROWS, HD),
            shape(BF16, 2 * ROWS + TILE, HD),
            shape(F32, 1, 128),
        ],
        [SM, SM] + [VM] * 4,
        [VM] * 6,
        [
            pltpu.VMEM((COMPACT, HD), F32),
            pltpu.VMEM((1024, HD), F32),
            pltpu.VMEM((1024, HD), F32),
        ],
        cost=pl.CostEstimate(flops=50000000, bytes_accessed=6000000, transcendentals=40000),
    )(info, bias, comp, o, z, xkv)


def bwd_kernel(info, comp, p_s, do_s, c_s, acc3, att, *refs):
    own, zs, core, own3, acc = refs[0], refs[1:4], refs[4], refs[5], refs[6]
    offs = [info[level] for level in range(LEVELS)]
    for level, parts in segments(info[4]):
        q, k, v = (load(comp.at[a], parts) for a in (2, 0, 1))
        p, do = load(p_s, parts), load(do_s, parts)
        ds = (p * (dot_nt(do, v) - twice(load(c_s, parts)))).astype(BF16)
        dq = dot_nn(ds, k) * SCALE
        both = dot_tn(
            jnp.concatenate([ds, p.astype(BF16)], axis=1),
            jnp.concatenate([q, do], axis=1),
        )
        dk = both[:256, :HD] * SCALE
        dv = both[256:, HD:]
        for which, value in enumerate((dq, dk, dv)):
            if level == 0:
                acc[which, pl.ds(parts[0][0], 256)] = value
                continue
            row = 0
            for start, size in parts:
                for i in range(size // TILE):
                    s = (start - BASE[level]) // (TILE * PER[level]) + i // PER[level]
                    rho = offs[level] + (1 << level) * (i % PER[level])
                    at = tile_at(s * ROWS + rho * TILE)
                    acc[which, at] = acc[which, at] + value[row : row + TILE]
                    row += TILE
    for s in range(8):
        at = tile_at(s * ROWS + offs[3] * TILE)
        part = slice(s * TILE, (s + 1) * TILE)
        for which in range(3):
            total = acc[which, at] + acc3[which, part]
            acc[which, at] = total
            if which > 0:
                own3[which - 1, part] = total
    for s, (dz, dc) in enumerate(SLOTS):
        home = core.at[dz] if dc else (zs[dz - 1].at[0] if dz else own)
        home[0] = att[s]
        for which in range(3):
            home[1 + which] = acc[which, s * ROWS : (s + 1) * ROWS].astype(BF16)


MSGS = [shape(BF16, 4, ROWS, HD)] + [shape(BF16, 2, 4, ROWS, HD)] * 3
CORES = shape(BF16, 4, 4, ROWS, HD)


def backward(info, comp, p, do, c, acc3, att):
    return call(
        bwd_kernel,
        MSGS + [CORES, shape(F32, 2, ROWS, HD)],
        [SM] + [VM] * 6,
        [VM] * 6,
        [pltpu.VMEM((3, 1024, HD), F32)],
        cost=pl.CostEstimate(flops=600000000, bytes_accessed=6000000, transcendentals=0),
    )(info, comp, p, do, c, acc3, att)


def full(*dims):
    return pl.BlockSpec(dims, lambda i, info: (0,) * len(dims))


def patch(kernel, outs, blocks, ins, in_blocks, info):
    count = len(blocks)
    return pl.pallas_call(
        kernel,
        out_shape=outs,
        grid_spec=pltpu.PrefetchScalarGridSpec(
            num_scalar_prefetch=1,
            grid=(1,),
            in_specs=[pl.BlockSpec(memory_space=pl.ANY)] * count + in_blocks,
            out_specs=blocks + [full(*x.shape) for x in outs[count:]],
        ),
        input_output_aliases={1 + n: n for n in range(count)},
        compiler_params=PARAMS,
    )(info, *ins)


def merge_kernel(info, *refs):
    own3, xin, bias = refs[5:8]
    own, zs, core, bias_out = refs[8], refs[9:12], refs[12], refs[13]
    terms = jnp.sum(xin[2 * ROWS :].astype(F32), axis=0, keepdims=True)
    bias_out[...] = bias[...] + terms
    for s, (dz, dc) in enumerate(SLOTS):
        at = slice(s * TILE, (s + 1) * TILE)
        for a in range(2):
            theirs = xin[a * ROWS + s * TILE : a * ROWS + (s + 1) * TILE]
            total = (own3[a, at] + theirs.astype(F32)).astype(BF16)
            if dc:
                core[dz, a] = total
            elif dz:
                zs[dz - 1][0, a] = total
            else:
                own[a] = total


def merge(info, msgs, own3, xin, bias):
    one = pl.BlockSpec((2, TILE, HD), lambda i, info: (1, info[3], 0))
    two = pl.BlockSpec((1, 2, TILE, HD), lambda i, info: (0, 1, info[3], 0))
    four = pl.BlockSpec((4, 2, TILE, HD), lambda i, info: (0, 1, info[3], 0))
    return patch(
        merge_kernel,
        MSGS + [CORES, shape(F32, 1, 128)],
        [one, two, two, two, four],
        [*msgs, own3, xin, bias],
        [full(2, ROWS, HD), full(2 * ROWS + TILE, HD), full(1, 128)],
        info,
    )


def relay_kernel(info, *refs):
    core, bias, theirs = refs[3:6]
    zs, total = refs[6:9], refs[9]
    for dz in range(1, 4):
        zs[dz - 1][0] = core[4 - dz]
    total[...] = bias[...] + theirs[...]


def relay(info, msgs, core, biases):
    half = pl.BlockSpec((1, 4, ROWS, HD), lambda i, info: (1, 0, 0, 0))
    return patch(
        relay_kernel,
        MSGS[1:] + [shape(F32, 1, 128)],
        [half] * 3,
        [*msgs, core, *biases],
        [full(*CORES.shape), full(1, 128), full(1, 128)],
        info,
    )


def unpack_kernel(info, *refs):
    own, core = refs[0], refs[4]
    zs = [refs[2], refs[1], refs[3]]
    outs = refs[5:9]
    e = info[4]
    order = row_order(True)
    for a in range(4):
        for dz, dc in SLOTS:
            home = zs[3 - dz if dc else dz - 1].at[dc] if dz else (core.at[0] if dc else own)
            at = head_at(dest_head(e, dz, dc))
            outs[a][:, at] = dot_nn(order, home[a]).astype(BF16)


def total_kernel(bias, out):
    total = jnp.sum(bias[...], axis=0, keepdims=True)
    for level in range(LEVELS):
        out[level : level + 1] = total[:, level * H : (level + 1) * H]


def bias_total(bias):
    return call(total_kernel, shape(F32, LEVELS, H), [VM], VM)(bias)


def unpack(info, own, zs, core):
    return call(
        unpack_kernel,
        [shape(BF16, ROWS, H * HD)] * 4,
        [SM] + [VM] * 5,
        [VM] * 4,
        cost=SHADOW,
    )(info, own, zs[1], zs[0], zs[2], core)


def local(queries, keys, values, cotangent, head_offsets, level_bias):
    def move(x, pairs):
        return lax.ppermute(x, "seq", pairs)

    packed = pack(head_offsets, keys, values, queries, cotangent)
    sent, info = packed[:8], packed[8]
    got = [sent[0]] + [None] * 7
    for slot in SEND:
        got[slot] = move(sent[slot], z_perm(*SLOTS[slot]))
    xkv = move(pick3(info, got), xor_perm(8))
    comp, p, o, z = forward(info, got)
    att, do, c, acc3, xout, bias = mixing(info, level_bias, comp, o, z, xkv)
    xin = move(xout, xor_perm(8))
    *msgs, own3 = backward(info, comp, p, do, c, acc3, att)
    own, *zs, core, bias = merge(info, msgs, own3, xin, bias)
    core = move(core, xor_perm(1))
    biases = [bias, move(bias, xor_perm(1))]
    *zs, bias = relay(info, zs, core, biases)
    zs = [move(x, back_perm(dz, 0)) for dz, x in zip((1, 2, 3), zs)]
    spread = jnp.broadcast_to(bias[:, : LEVELS * H], (64, LEVELS * H))
    bias = lax.all_to_all(
        spread, ("grp", "seq"), 0, 0, axis_index_groups=GROUPS, tiled=True
    )
    outs = unpack(info, own, zs, core)
    outs, bias = lax.optimization_barrier((outs, bias))
    return (*outs, bias_total(bias))


def solution(mesh):
    rows = P(("grp", "seq"), None)
    return jax.shard_map(
        local,
        mesh=mesh,
        in_specs=(rows, rows, rows, rows, P(), P()),
        out_specs=(rows, rows, rows, rows, P()),
        check_vma=False,
    )
```
